512 devices in a mesh: ctx: 64 (over x, z, core), tp: 8 (over y).
Axes of the slice: x: 4, y: 8, z: 8, core: 2. Of those that a mesh axis runs over, the one named last changes fastest.
Arguments:
- queries: bfloat16 [16384, 4096], P(('ctx', 'tp')), may hold values from -8 to 8
- keys: bfloat16 [16384, 1024], P(('ctx', 'tp')), may hold values from -8 to 8
- values: bfloat16 [16384, 1024], P(('ctx', 'tp')), may hold values from -6 to 6
- grad_out: bfloat16 [16384, 4096], P(('ctx', 'tp')), may hold values from -6 to 6
- doc_lengths: int32 [24], replicated, may hold values from 1 to 2048, 16384 in all
Outputs:
- grad_queries: bfloat16 [16384, 4096], P(('ctx', 'tp'))
- grad_keys: bfloat16 [16384, 1024], P(('ctx', 'tp'))
- grad_values: bfloat16 [16384, 1024], P(('ctx', 'tp'))
The draws below stay inside these ranges and needn't reach their ends.
Inputs may be any that keep to these rules, and one draw needn't show every extreme that they name: `doc_lengths`: whole documents in order; the lengths sum to 16384 and the longest has exactly 2048 tokens.
All inputs are finite; a program needn't handle non-finite values.
Results may differ from the reference program's by a relative error of at most 0.02.
Values may be sent and summed in bfloat16 or wider, within the bound.
A program may use at most 64 MiB of HBM per device.

```python
import math
import jax
import jax.numpy as jnp
import numpy as np
from jax import lax

HEADS = 32
KV_HEADS = 8
HEAD = 128
TOK_DEV = 256
TOKENS = 16384
DOC_MAX = 2048
DOCS = 24


def draw_queries(key, part):
    key = jax.random.fold_in(key, 3)
    first = jax.random.fold_in(key, 0)
    base = jnp.clip(jax.random.normal(first, (TOKENS, HEADS * HEAD), jnp.float32), -6.0, 6.0)
    return base.astype(jnp.bfloat16)


def draw_keys(key, part):
    key = jax.random.fold_in(key, 5)
    first = jax.random.fold_in(key, 0)
    base = jnp.clip(jax.random.normal(first, (TOKENS, KV_HEADS * HEAD), jnp.float32), -6.0, 6.0)
    return base.astype(jnp.bfloat16)


def block_scale(rng, extent, pieces, smallest, top_value):
    loudness, own = 1.0, jax.random.fold_in(rng, 6)
    for axis_at, shards_of in pieces:
        heights = jnp.exp(jax.random.uniform(jax.random.fold_in(own, axis_at), (shards_of,), jnp.float32, smallest / len(pieces), top_value / len(pieces)))
        loudness = loudness * jnp.repeat(heights, extent[axis_at] // shards_of).reshape([-1 if axis == axis_at else 1 for axis in range(len(extent))])
    return loudness


def length_profile(number_of, total, limit, skew):
    loads = [(1 << 20) // math.isqrt(grade ** skew) + 1 for grade in range(2, number_of + 1)]
    rest, holding = total - limit - (number_of - 1), [1] * (number_of - 1)
    while rest > 0:
        free = [i for i in range(number_of - 1) if holding[i] < limit]
        mass, budget = sum([loads[i] for i in free]), rest
        for i in free:
            more = min(limit - holding[i], max(1, budget * loads[i] // mass), rest)
            holding[i] = holding[i] + more
            rest = rest - more
    return np.array([limit] + holding)


def uneven(rng, amount, total, reach, lean):
    if amount == 2:
        one = jax.random.randint(rng, (), max(1, total - reach), min(reach, total - 1) + 1)
        return jnp.stack([one, total - one])
    sizes = jnp.asarray(length_profile(amount, total, reach, lean), jnp.int32)
    pairs = (amount - 1) // 2
    source_of, sink = sizes[1:1 + 2 * pairs:2], sizes[2:2 + 2 * pairs:2]
    slack = jnp.minimum(source_of - 1, reach - sink)
    moved = jax.random.randint(jax.random.fold_in(rng, 1), (pairs,), 0, 1 << 20) % (slack + 1)
    sizes = sizes.at[1:1 + 2 * pairs:2].set(source_of - moved).at[2:2 + 2 * pairs:2].set(sink + moved)
    return sizes[jax.random.permutation(jax.random.fold_in(rng, 2), amount)]


def scatter_about(rng, extent, scale, limit, cuts=(), kind=jnp.bfloat16):
    array = scale * jax.random.normal(rng, extent, jnp.float32)
    if cuts:
        array = array * block_scale(rng, extent, cuts, -0.22, 0.18)
    return jnp.clip(array, -limit, limit).astype(kind)


def setup_inputs(seed: int = 0) -> dict:
    arg_keys = jax.random.split(jax.random.key(seed), 6)
    return {
        "queries": draw_queries(jax.random.fold_in(arg_keys[5], 71), 0),
        "keys": draw_keys(jax.random.fold_in(arg_keys[5], 71), 0),
        "values": scatter_about(arg_keys[2], (TOKENS, KV_HEADS * HEAD), 1.0, 6.0, ((0, 512),)),
        "grad_out": scatter_about(arg_keys[3], (TOKENS, HEADS * HEAD), 1.0, 6.0, ((0, 512),)),
        "doc_lengths": uneven(arg_keys[4], DOCS, TOKENS, DOC_MAX, 2).astype(jnp.int32),
    }


def document_of(positions, doc_lengths):
    ends = jnp.cumsum(doc_lengths).astype(jnp.int32)
    found = jnp.sum((positions[:, None] >= ends[None, :]).astype(jnp.int32), axis=1)
    return jnp.where(positions >= 0, found, -1).astype(jnp.int32)


def reference(queries, keys, values, grad_out, doc_lengths):
    group = HEADS // KV_HEADS
    factor = HEAD ** -0.5
    window = DOC_MAX + TOK_DEV
    query_four = queries.reshape(TOKENS, KV_HEADS, group, HEAD)
    cotangent = grad_out.reshape(TOKENS, KV_HEADS, group, HEAD)
    front = jnp.zeros((DOC_MAX, KV_HEADS, HEAD), keys.dtype)
    key_pad = jnp.concatenate([front, keys.reshape(TOKENS, KV_HEADS, HEAD)], axis=0)
    value_pad = jnp.concatenate([front, values.reshape(TOKENS, KV_HEADS, HEAD)], axis=0)
    key_positions = jnp.arange(TOKENS + DOC_MAX, dtype=jnp.int32) - DOC_MAX
    key_docs = document_of(key_positions, doc_lengths)
    query_positions = jnp.arange(TOKENS, dtype=jnp.int32)
    query_docs = document_of(query_positions, doc_lengths)

    def block(carry, index):
        grad_key_acc, grad_value_acc = carry
        start = (index * TOK_DEV).astype(jnp.int32)
        query_blk = lax.dynamic_slice_in_dim(query_four, start, TOK_DEV, 0).astype(jnp.float32)
        cot_blk = lax.dynamic_slice_in_dim(cotangent, start, TOK_DEV, 0).astype(jnp.float32)
        key_blk = lax.dynamic_slice_in_dim(key_pad, start, window, 0).astype(jnp.float32)
        value_blk = lax.dynamic_slice_in_dim(value_pad, start, window, 0).astype(jnp.float32)
        qpos = lax.dynamic_slice_in_dim(query_positions, start, TOK_DEV, 0)
        qdoc = lax.dynamic_slice_in_dim(query_docs, start, TOK_DEV, 0)
        kpos = lax.dynamic_slice_in_dim(key_positions, start, window, 0)
        kdoc = lax.dynamic_slice_in_dim(key_docs, start, window, 0)
        allowed = (qdoc[:, None] == kdoc[None, :]) & (kpos[None, :] <= qpos[:, None]) & (kdoc[None, :] >= 0)
        scores = jnp.einsum('qngd,knd->ngqk', query_blk, key_blk) * factor
        masked = jnp.where(allowed, scores, -1e30)
        top = jnp.max(masked, axis=-1, keepdims=True)
        total = jnp.sum(jnp.where(allowed, jnp.exp(masked - top), 0.0), axis=-1, keepdims=True)
        lse = top + jnp.log(total)
        probs = jnp.where(allowed, jnp.exp(masked - lse), 0.0)
        dprobs = jnp.einsum('qngd,knd->ngqk', cot_blk, value_blk)
        delta = jnp.sum(probs * dprobs, axis=-1, keepdims=True)
        probs_b = probs.astype(jnp.bfloat16).astype(jnp.float32)
        dscores_b = (probs * (dprobs - delta)).astype(jnp.bfloat16).astype(jnp.float32)
        grad_q = (jnp.einsum('ngqk,knd->qngd', dscores_b, key_blk) * factor).astype(jnp.bfloat16)
        grad_k = jnp.einsum('ngqk,qngd->knd', dscores_b, query_blk) * factor
        grad_v = jnp.einsum('ngqk,qngd->knd', probs_b, cot_blk)
        old_k = lax.dynamic_slice_in_dim(grad_key_acc, start, window, 0)
        old_v = lax.dynamic_slice_in_dim(grad_value_acc, start, window, 0)
        grad_key_acc = lax.dynamic_update_slice_in_dim(grad_key_acc, old_k + grad_k, start, 0)
        grad_value_acc = lax.dynamic_update_slice_in_dim(grad_value_acc, old_v + grad_v, start, 0)
        return (grad_key_acc, grad_value_acc), grad_q

    empty = jnp.zeros((TOKENS + DOC_MAX, KV_HEADS, HEAD), jnp.float32)
    (grad_key_acc, grad_value_acc), grad_q = lax.scan(block, (empty, empty), jnp.arange(TOKENS // TOK_DEV, dtype=jnp.int32))
    grad_queries = grad_q.reshape(TOKENS, HEADS * HEAD)
    grad_keys = grad_key_acc[DOC_MAX:].reshape(TOKENS, KV_HEADS * HEAD).astype(jnp.bfloat16)
    grad_values = grad_value_acc[DOC_MAX:].reshape(TOKENS, KV_HEADS * HEAD).astype(jnp.bfloat16)
    return grad_queries, grad_keys, grad_values
```

```python
import functools

import jax
import jax.numpy as jnp
from jax import lax
from jax.experimental import pallas as pl
from jax.experimental.pallas import tpu as pltpu
from jax.sharding import PartitionSpec as P

HEAD = 128
FAR = 4
MESH = pl.DeviceIdType.MESH
LOG2E = 1.4426950408889634
LOW = -1e30

NT = (((1,), (1,)), ((), ()))


def dot(a, b, dims=(((1,), (0,)), ((), ()))):
    return lax.dot_general(a, b, dims, preferred_element_type=jnp.float32)


def kernel(
    q_in, k_in, v_in, c_in, lengths,
    gq_out, gk_out, gv_out,
    q_blk, c_blk, k_win, v_win, weights, dprobs, tops, starts,
    dq_acc, dq_out, own, sib_out, sib_in, back_out, back_in,
    in_send, in_recv, fwd_send, fwd_recv, pair_send, pair_recv,
    back_send, back_recv, term_send, term_recv, out_send, out_recv,
):
    n = lax.axis_size("tp")
    ring = lax.axis_size("ctx")
    me = lax.axis_index("ctx")
    y = lax.axis_index("tp")
    core = lax.rem(me, 2)
    after = lax.rem(me + 2, ring)
    before = lax.rem(me + ring - 2, ring)
    twin = me + 1 - 2 * core
    rows = q_in.shape[0]
    block = rows * n
    group = q_blk.shape[1] // HEAD
    wide = group * HEAD
    factor = HEAD ** -0.5
    scale = factor * LOG2E
    mine = 1 - core

    barrier = pltpu.get_barrier_semaphore()

    def greet(o, carry):
        pl.semaphore_signal(
            barrier, inc=1, device_id=(me, lax.rem(y + o, n)), device_id_type=MESH
        )
        return carry

    lax.fori_loop(1, n, greet, 0)
    for other in (after, before, twin):
        pl.semaphore_signal(barrier, inc=1, device_id=(other, y), device_id_type=MESH)
    pl.semaphore_wait(barrier, n + 2)

    here = pl.ds(pl.multiple_of(y * rows, rows), rows)

    def spread(index, src, width, dst):
        def send(o, carry):
            to = lax.rem(y + o, n)
            pltpu.make_async_remote_copy(
                src_ref=src.at[:, pl.ds(pl.multiple_of(to * width, width), width)],
                dst_ref=dst,
                send_sem=in_send.at[index],
                recv_sem=in_recv.at[index],
                device_id=(me, to),
                device_id_type=MESH,
            ).start()
            return carry

        lax.fori_loop(1, n, send, 0)
        pltpu.make_async_copy(
            src.at[:, pl.ds(pl.multiple_of(y * width, width), width)], dst, in_recv.at[index]
        ).start()

    spread(0, k_in, HEAD, k_win.at[mine, here, :])
    spread(1, v_in, HEAD, v_win.at[mine, here, :])
    spread(2, q_in, wide, q_blk.at[here, :])
    spread(3, c_in, wide, c_blk.at[here, :])

    def got(ref, sem):
        pltpu.make_async_copy(ref, ref, sem).wait()

    def forward(index, win, step):
        at = 2 * step + mine
        return pltpu.make_async_remote_copy(
            src_ref=win.at[at],
            dst_ref=win.at[at + 2],
            send_sem=fwd_send.at[step, index],
            recv_sem=fwd_recv.at[step, index],
            device_id=(after, y),
            device_id_type=MESH,
        )

    def share(index, win, step):
        at = 2 * step + mine
        return pltpu.make_async_remote_copy(
            src_ref=win.at[at],
            dst_ref=win.at[at],
            send_sem=pair_send.at[step, index],
            recv_sem=pair_recv.at[step, index],
            device_id=(twin, y),
            device_id_type=MESH,
        )

    wins = (k_win, v_win)
    for index, win in enumerate(wins):
        got(win.at[mine], in_recv.at[index])
        forward(index, win, 0).start()
        share(index, win, 0).start()

    position = me * block + lax.broadcasted_iota(jnp.int32, (1, block), 1)
    begin = jnp.zeros((1, block), jnp.int32)
    end = jnp.int32(0)
    for d in range(lengths.shape[0]):
        end = end + lengths[d]
        begin = jnp.where(position >= end, end, begin)
    starts[...] = begin
    key_row = lax.broadcasted_iota(jnp.int32, (block, block), 0)
    query_lane = lax.broadcasted_iota(jnp.int32, (block, block), 1)

    for step in range(1, FAR):
        for index, win in enumerate(wins):
            forward(index, win, step - 1).wait_recv()
            forward(index, win, step).start()
            share(index, win, step).start()

    got(q_blk, in_recv.at[2])
    got(c_blk, in_recv.at[3])

    def columns(h):
        return slice(h * HEAD, (h + 1) * HEAD)

    def scan_block(far, carry, diagonal):
        at = far + mine
        k = k_win[at]
        v = v_win[at]
        allowed = key_row >= starts[...] - (me - far) * block
        if diagonal:
            allowed = allowed & (key_row <= query_lane)
        new = []
        for h in range(group):
            s = dot(k, q_blk[:, columns(h)], NT)
            dp = dot(v, c_blk[:, columns(h)], NT)
            s = jnp.where(allowed, s, LOW)
            top = jnp.max(s, axis=0, keepdims=True)
            if not diagonal:
                top = jnp.maximum(top, carry[h][0])
            e = jnp.exp2(s * scale - top * scale)
            total = jnp.sum(e, axis=0, keepdims=True)
            weighted = jnp.sum(e * dp, axis=0, keepdims=True)
            if not diagonal:
                old, old_total, old_weighted = carry[h]
                shrink = jnp.exp2((old - top) * scale)
                total = total + old_total * shrink
                weighted = weighted + old_weighted * shrink
            weights[far * group + h] = e
            dprobs[far * group + h] = dp
            tops[far * group + h] = top
            new.append((top, total, weighted))
        return tuple(new)

    stats = scan_block(0, None, True)
    for step in range(FAR):
        for index, win in enumerate(wins):
            share(index, win, step).wait_recv()
    stats = lax.fori_loop(1, 2 * FAR - 1, lambda far, c: scan_block(far, c, False), stats)
    for index, win in enumerate(wins):
        forward(index, win, FAR - 1).wait_recv()
        share(index, win, FAR).start()
    for index, win in enumerate(wins):
        share(index, win, FAR).wait_recv()
    stats = lax.fori_loop(2 * FAR - 1, 2 * FAR + 1, lambda far, c: scan_block(far, c, False), stats)

    dq_acc[...] = jnp.zeros_like(dq_acc)

    def terms(far):
        at = far + mine
        k_t = k_win[at].T
        dk = jnp.zeros((block, HEAD), jnp.float32)
        dv = jnp.zeros((block, HEAD), jnp.float32)
        for h in range(group):
            top, total, weighted = stats[h]
            inv = 1.0 / total
            shrink = jnp.exp2((tops[far * group + h] - top) * scale) * inv
            p = weights[far * group + h] * shrink
            ds = (p * (dprobs[far * group + h] - weighted * inv)).astype(jnp.bfloat16)
            dv = dv + dot(p.astype(jnp.bfloat16), c_blk[:, columns(h)])
            dk = dk + dot(ds, q_blk[:, columns(h)])
            dq_acc[h] += dot(k_t, ds)
        return dk, dv

    def hand_over(index, step):
        return pltpu.make_async_remote_copy(
            src_ref=sib_out.at[step, index],
            dst_ref=sib_in.at[step, index],
            send_sem=term_send.at[step, index],
            recv_sem=term_recv.at[step, index],
            device_id=(twin, y),
            device_id_type=MESH,
        )

    def back(index, step):
        return pltpu.make_async_remote_copy(
            src_ref=back_out.at[step, index],
            dst_ref=back_in.at[step - 1, index],
            send_sem=back_send.at[step - 1, index],
            recv_sem=back_recv.at[step - 1, index],
            device_id=(before, y),
            device_id_type=MESH,
        )

    def gives(step):
        return (step >= 1 - core) & (step <= FAR - core)

    def takes(step):
        return (step >= core) & (step <= FAR - 1 + core)

    def make_terms(step):
        @pl.when(gives(step))
        def _():
            for index, term in enumerate(terms(2 * step - 1 + 2 * core)):
                sib_out[step, index] = term.astype(jnp.bfloat16)
                hand_over(index, step).start()

        for index, term in enumerate(terms(2 * step)):
            own[step, index] = term

    def collect(step):
        for index in range(2):
            @pl.when(takes(step))
            def _():
                hand_over(index, step).wait_recv()
                own[step, index] += sib_in[step, index].astype(jnp.float32)

            @pl.when(step < FAR)
            def _():
                back(index, step + 1).wait_recv()
                own[step, index] += back_in[step, index].astype(jnp.float32)

            if index == 0:
                sums = own[step, index] * jnp.where(step == 0, factor, 1.0)
            else:
                sums = own[step, index]
            back_out[step, index] = sums.astype(jnp.bfloat16)

            @pl.when(step > 0)
            def _():
                back(index, step).start()

    def make_step(i, carry):
        step = FAR - i
        make_terms(step)

        @pl.when(step == FAR)
        def _():
            collect(step)

        return carry

    lax.fori_loop(0, FAR + 1, make_step, 0)

    def deliver(index, src, width, dst):
        to_columns = dst.at[:, pl.ds(pl.multiple_of(y * width, width), width)]

        def send(o, carry):
            to = lax.rem(y + o, n)
            pltpu.make_async_remote_copy(
                src_ref=src.at[pl.ds(pl.multiple_of(to * rows, rows), rows), :],
                dst_ref=to_columns,
                send_sem=out_send.at[index],
                recv_sem=out_recv.at[index],
                device_id=(me, to),
                device_id_type=MESH,
            ).start()
            return carry

        lax.fori_loop(1, n, send, 0)
        pltpu.make_async_copy(src.at[here, :], to_columns, out_recv.at[index]).start()

    for h in range(group):
        dq_out[:, columns(h)] = (dq_acc[h] * factor).T.astype(jnp.bfloat16)
    deliver(0, dq_out, wide, gq_out)

    def collect_step(i, carry):
        collect(FAR - 1 - i)
        return carry

    lax.fori_loop(0, FAR, collect_step, 0)
    deliver(1, back_out.at[0, 0], HEAD, gk_out)
    deliver(2, back_out.at[0, 1], HEAD, gv_out)

    for index, ref in enumerate((gq_out, gk_out, gv_out)):
        got(ref, out_recv.at[index])

    for index, (ref, width) in enumerate(((k_in, HEAD), (v_in, HEAD), (q_in, wide), (c_in, wide))):
        got(ref.at[:, pl.ds(0, (n - 1) * width)], in_send.at[index])
    for index, ref in enumerate((dq_out, back_out.at[0, 0], back_out.at[0, 1])):
        got(ref.at[pl.ds(0, (n - 1) * rows), :], out_send.at[index])
    for index, win in enumerate(wins):
        for step in range(FAR):
            forward(index, win, step).wait_send()
            back(index, step + 1).wait_send()
        for step in range(FAR + 1):
            share(index, win, step).wait_send()

            @pl.when(gives(step))
            def _():
                hand_over(index, step).wait_send()


def shards(queries, keys, values, grad_out, doc_lengths):
    n = lax.axis_size("tp")
    rows = queries.shape[0]
    block = rows * n
    wide = queries.shape[1] // n
    group = wide // HEAD
    blocks = 2 * FAR + 1
    bf16, f32 = jnp.bfloat16, jnp.float32
    vmem = pltpu.VMEM
    dma = pltpu.SemaphoreType.DMA
    any_spec = pl.BlockSpec(memory_space=pl.ANY)
    return pl.pallas_call(
        kernel,
        out_shape=[
            jax.ShapeDtypeStruct(queries.shape, bf16),
            jax.ShapeDtypeStruct(keys.shape, bf16),
            jax.ShapeDtypeStruct(values.shape, bf16),
        ],
        in_specs=[any_spec] * 4 + [pl.BlockSpec(memory_space=pltpu.SMEM)],
        out_specs=[any_spec] * 3,
        scratch_shapes=[
            vmem((block, wide), bf16),
            vmem((block, wide), bf16),
            vmem((2 * FAR + 2, block, HEAD), bf16),
            vmem((2 * FAR + 2, block, HEAD), bf16),
            vmem((blocks * group, block, block), f32),
            vmem((blocks * group, block, block), f32),
            vmem((blocks * group, 1, block), f32),
            vmem((1, block), jnp.int32),
            vmem((group, HEAD, block), f32),
            vmem((block, wide), bf16),
            vmem((FAR + 1, 2, block, HEAD), f32),
            vmem((FAR + 1, 2, block, HEAD), bf16),
            vmem((FAR + 1, 2, block, HEAD), bf16),
            vmem((FAR + 1, 2, block, HEAD), bf16),
            vmem((FAR, 2, block, HEAD), bf16),
            dma((4,)),
            dma((4,)),
            dma((FAR, 2)),
            dma((FAR, 2)),
            dma((FAR + 1, 2)),
            dma((FAR + 1, 2)),
            dma((FAR, 2)),
            dma((FAR, 2)),
            dma((FAR + 1, 2)),
            dma((FAR + 1, 2)),
            dma((3,)),
            dma((3,)),
        ],
        compiler_params=pltpu.CompilerParams(
            collective_id=0, has_side_effects=True, vmem_limit_bytes=48 * 2**20
        ),
    )(queries, keys, values, grad_out, doc_lengths)


def solution(mesh):
    placed = P(("ctx", "tp"), None)
    return jax.shard_map(
        shards,
        mesh=mesh,
        in_specs=(placed,) * 4 + (P(),),
        out_specs=(placed,) * 3,
        check_vma=False,
    )
```

```python
import functools

import jax
import jax.numpy as jnp
from jax import lax
from jax.experimental import pallas as pl
from jax.experimental.pallas import tpu as pltpu
from jax.sharding import PartitionSpec as P

HEAD = 128
FAR = 4
HALVES = 2
MESH = pl.DeviceIdType.MESH
LOG2E = 1.4426950408889634
LOW = -1e30

NT = (((1,), (1,)), ((), ()))


def dot(a, b, dims=(((1,), (0,)), ((), ()))):
    return lax.dot_general(a, b, dims, preferred_element_type=jnp.float32)


def kernel(
    q_in, k_in, v_in, c_in, lengths,
    gq_out, near_k, near_v, far_k, far_v,
    q_stage, k_stage, v_stage, c_stage,
    q_blk, c_blk, k_win, v_win, weights, dprobs, tops, starts,
    dq_acc, dq_out, own, sib_out, sib_in, back_out, back_in,
    stage_sem, in_send, in_recv, fwd_send, fwd_recv, pair_send, pair_recv,
    back_send, back_recv, term_send, term_recv, out_send, out_recv,
):
    n = lax.axis_size("tp")
    ring = lax.axis_size("ctx")
    me = lax.axis_index("ctx")
    y = lax.axis_index("tp")
    core = lax.rem(me, 2)
    after = lax.rem(me + 2, ring)
    before = lax.rem(me + ring - 2, ring)
    twin = me + 1 - 2 * core
    rows = q_in.shape[0]
    block = rows * n
    half = block // HALVES
    group = dq_out.shape[1] // HEAD
    wide = group * HEAD
    factor = HEAD ** -0.5
    scale = factor * LOG2E
    mine = 1 - core
    offsets = sorted(range(1, n), key=lambda o: -min(o, n - o))

    barrier = pltpu.get_barrier_semaphore()
    for o in offsets:
        pl.semaphore_signal(
            barrier, inc=1, device_id=(me, lax.rem(y + o, n)), device_id_type=MESH
        )
    for other in (after, before, twin):
        pl.semaphore_signal(barrier, inc=1, device_id=(other, y), device_id_type=MESH)

    staged = ((k_in, k_stage), (v_in, v_stage), (q_in, q_stage), (c_in, c_stage))
    for index, (src, dst) in enumerate(staged):
        pltpu.make_async_copy(src, dst, stage_sem.at[index]).start()

    position = me * block + lax.broadcasted_iota(jnp.int32, (1, block), 1)
    begin = jnp.zeros((1, block), jnp.int32)
    end = jnp.int32(0)
    for d in range(lengths.shape[0]):
        end = end + lengths[d]
        begin = jnp.where(position >= end, end, begin)
    starts[...] = begin
    key_row = lax.broadcasted_iota(jnp.int32, (block, block), 0)
    query_lane = lax.broadcasted_iota(jnp.int32, (block, block), 1)

    for index, (src, dst) in enumerate(staged):
        pltpu.make_async_copy(src, dst, stage_sem.at[index]).wait()
    pl.semaphore_wait(barrier, n + 2)

    here = pl.ds(pl.multiple_of(y * rows, rows), rows)

    def spread(index, src, stride, width, shift, dst):
        def of(p):
            return src.at[:, pl.ds(pl.multiple_of(p * stride + shift, HEAD), width)]

        for o in offsets:
            to = lax.rem(y + o, n)
            pltpu.make_async_remote_copy(
                src_ref=of(to),
                dst_ref=dst,
                send_sem=in_send.at[index],
                recv_sem=in_recv.at[index],
                device_id=(me, to),
                device_id_type=MESH,
            ).start()
        pltpu.make_async_copy(of(y), dst, in_recv.at[index]).start()

    pair = wide // 2
    spread(0, k_stage, HEAD, HEAD, 0, k_win.at[mine, here, :])
    spread(1, v_stage, HEAD, HEAD, 0, v_win.at[mine, here, :])
    for side in range(2):
        spread(2 + 2 * side, q_stage, wide, pair, side * pair, q_blk.at[side, here, :])
        spread(3 + 2 * side, c_stage, wide, pair, side * pair, c_blk.at[side, here, :])

    def got(ref, sem):
        pltpu.make_async_copy(ref, ref, sem).wait()

    wins = (k_win, v_win)
    pieces = [(index, part) for index in range(2) for part in range(HALVES)]

    def forward(piece, step):
        index, part = piece
        at = 2 * step + mine
        span = pl.ds(part * half, half)
        return pltpu.make_async_remote_copy(
            src_ref=wins[index].at[at, span],
            dst_ref=wins[index].at[at + 2, span],
            send_sem=fwd_send.at[step, index, part],
            recv_sem=fwd_recv.at[step, index, part],
            device_id=(after, y),
            device_id_type=MESH,
        )

    def share(piece, step):
        index, part = piece
        at = 2 * step + mine
        span = pl.ds(part * half, half)
        return pltpu.make_async_remote_copy(
            src_ref=wins[index].at[at, span],
            dst_ref=wins[index].at[at, span],
            send_sem=pair_send.at[step, index, part],
            recv_sem=pair_recv.at[step, index, part],
            device_id=(twin, y),
            device_id_type=MESH,
        )

    for index, win in enumerate(wins):
        got(win.at[mine], in_recv.at[index])
        for part in range(HALVES):
            forward((index, part), 0).start()
        for part in range(HALVES):
            share((index, part), 0).start()

    for step in range(1, FAR):
        for piece in pieces:
            forward(piece, step - 1).wait_recv()
            forward(piece, step).start()
            share(piece, step).start()

    def columns(h):
        return slice((h % 2) * HEAD, (h % 2 + 1) * HEAD)

    def queries_of(h):
        return q_blk[h // 2, :, columns(h)]

    def cotangents_of(h):
        return c_blk[h // 2, :, columns(h)]

    def scan_block(far, carry, heads, diagonal=False):
        at = far + mine
        k = k_win[at]
        v = v_win[at]
        allowed = key_row >= starts[...] - (me - far) * block
        if diagonal:
            allowed = allowed & (key_row <= query_lane)
        new = []
        for j, h in enumerate(heads):
            s = dot(k, queries_of(h), NT)
            dp = dot(v, cotangents_of(h), NT)
            s = jnp.where(allowed, s, LOW)
            top = jnp.max(s, axis=0, keepdims=True)
            if not diagonal:
                top = jnp.maximum(top, carry[j][0])
            e = jnp.exp2(s * scale - top * scale)
            total = jnp.sum(e, axis=0, keepdims=True)
            weighted = jnp.sum(e * dp, axis=0, keepdims=True)
            if not diagonal:
                old, old_total, old_weighted = carry[j]
                shrink = jnp.exp2((old - top) * scale)
                total = total + old_total * shrink
                weighted = weighted + old_weighted * shrink
            weights[far * group + h] = e
            dprobs[far * group + h] = dp
            tops[far * group + h] = top
            new.append((top, total, weighted))
        return tuple(new)

    def scan(first, last, carry, heads):
        return lax.fori_loop(first, last, lambda far, c: scan_block(far, c, heads), carry)

    sides = (tuple(range(group // 2)), tuple(range(group // 2, group)))
    got(q_blk.at[0], in_recv.at[2])
    got(c_blk.at[0], in_recv.at[3])
    stats = [scan_block(0, None, sides[0], True), None]
    for step in range(FAR):
        for piece in pieces:
            share(piece, step).wait_recv()
    stats[0] = scan(1, 2 * FAR - 1, stats[0], sides[0])
    for piece in pieces:
        forward(piece, FAR - 1).wait_recv()
        share(piece, FAR).start()
    got(q_blk.at[1], in_recv.at[4])
    got(c_blk.at[1], in_recv.at[5])
    stats[1] = scan_block(0, None, sides[1], True)
    stats[1] = scan(1, 2 * FAR - 1, stats[1], sides[1])
    for piece in pieces:
        share(piece, FAR).wait_recv()
    for side in range(2):
        stats[side] = scan(2 * FAR - 1, 2 * FAR + 1, stats[side], sides[side])
    stats = stats[0] + stats[1]

    dq_acc[...] = jnp.zeros_like(dq_acc)

    def terms(far):
        at = far + mine
        k_t = k_win[at].T
        dk = jnp.zeros((block, HEAD), jnp.float32)
        dv = jnp.zeros((block, HEAD), jnp.float32)
        for h in range(group):
            top, total, weighted = stats[h]
            inv = 1.0 / total
            shrink = jnp.exp2((tops[far * group + h] - top) * scale) * inv
            p = weights[far * group + h] * shrink
            ds = (p * (dprobs[far * group + h] - weighted * inv)).astype(jnp.bfloat16)
            dv = dv + dot(p.astype(jnp.bfloat16), cotangents_of(h))
            dk = dk + dot(ds, queries_of(h))
            dq_acc[h] += dot(k_t, ds)
        return dk, dv

    def hand_over(index, step):
        return pltpu.make_async_remote_copy(
            src_ref=sib_out.at[step, index],
            dst_ref=sib_in.at[step, index],
            send_sem=term_send.at[step, index],
            recv_sem=term_recv.at[step, index],
            device_id=(twin, y),
            device_id_type=MESH,
        )

    def back(piece, step):
        index, part = piece
        span = pl.ds(part * half, half)
        return pltpu.make_async_remote_copy(
            src_ref=back_out.at[step, index, span],
            dst_ref=back_in.at[step - 1, index, span],
            send_sem=back_send.at[step - 1, index, part],
            recv_sem=back_recv.at[step - 1, index, part],
            device_id=(before, y),
            device_id_type=MESH,
        )

    def gives(step):
        return (step >= 1 - core) & (step <= FAR - core)

    def takes(step):
        return (step >= core) & (step <= FAR - 1 + core)

    def make_terms(step):
        @pl.when(gives(step))
        def _():
            for index, term in enumerate(terms(2 * step - 1 + 2 * core)):
                sib_out[step, index] = term.astype(jnp.bfloat16)
                hand_over(index, step).start()

        for index, term in enumerate(terms(2 * step)):
            own[step, index] = term

    def take(step):
        @pl.when(takes(step))
        def _():
            for index in range(2):
                hand_over(index, step).wait_recv()
                own[step, index] += sib_in[step, index].astype(jnp.float32)

    def make_step(i, carry):
        step = FAR - i
        make_terms(step)

        @pl.when(step == FAR)
        def _():
            take(step)
            for index, part in pieces:
                span = pl.ds(part * half, half)
                back_out[step, index, span] = own[step, index, span].astype(jnp.bfloat16)
                back((index, part), step).start()

        return carry

    lax.fori_loop(0, FAR + 1, make_step, 0)

    mine_there = {
        HEAD: pl.ds(pl.multiple_of(y * HEAD, HEAD), HEAD),
        wide: pl.ds(pl.multiple_of(y * wide, wide), wide),
    }

    def deliver(index, src, width, dst, to_ctx, others):
        for o in others:
            to = lax.rem(y + o, n)
            pltpu.make_async_remote_copy(
                src_ref=src.at[pl.ds(pl.multiple_of(to * rows, rows), rows), :],
                dst_ref=dst.at[:, mine_there[width]],
                send_sem=out_send.at[index],
                recv_sem=out_recv.at[index],
                device_id=(to_ctx, to),
                device_id_type=MESH,
            ).start()
        if 0 not in others:
            pltpu.make_async_copy(
                src.at[here, :], dst.at[:, mine_there[width]], out_recv.at[index]
            ).start()

    for h in range(group):
        dq_out[:, h * HEAD : (h + 1) * HEAD] = (dq_acc[h] * factor).T.astype(jnp.bfloat16)
    deliver(0, dq_out, wide, gq_out, me, offsets)
    take(0)
    for index, dst in enumerate((near_k, near_v)):
        back_out[0, index] = own[0, index].astype(jnp.bfloat16)
        deliver(1 + index, back_out.at[0, index], HEAD, dst, me, offsets)

    for step in range(FAR - 1, 0, -1):
        take(step)
        for index, part in pieces:
            span = pl.ds(part * half, half)
            back((index, part), step + 1).wait_recv()
            sums = own[step, index, span] + back_in[step, index, span].astype(jnp.float32)
            back_out[step, index, span] = sums.astype(jnp.bfloat16)
            if step > 1:
                back((index, part), step).start()
            elif part == HALVES - 1:
                deliver(
                    3 + index, back_out.at[1, index], HEAD, (far_k, far_v)[index],
                    before, offsets + [0],
                )

    for index, ref in enumerate((gq_out, near_k, near_v, far_k, far_v)):
        got(ref, out_recv.at[index])

    sent = ((k_in, HEAD), (v_in, HEAD), (q_in, pair), (c_in, pair), (q_in, pair), (c_in, pair))
    for index, (ref, width) in enumerate(sent):
        got(ref.at[:, pl.ds(0, (n - 1) * width)], in_send.at[index])
    for index, ref in enumerate((dq_out, back_out.at[0, 0], back_out.at[0, 1])):
        got(ref.at[pl.ds(0, (n - 1) * rows), :], out_send.at[index])
    for index in range(2):
        got(back_out.at[1, index], out_send.at[3 + index])
    for piece in pieces:
        for step in range(FAR):
            forward(piece, step).wait_send()
            if step:
                back(piece, step + 1).wait_send()
        for step in range(FAR + 1):
            share(piece, step).wait_send()
    for step in range(FAR + 1):
        @pl.when(gives(step))
        def _():
            for index in range(2):
                hand_over(index, step).wait_send()


def shards(queries, keys, values, grad_out, doc_lengths):
    n = lax.axis_size("tp")
    rows = queries.shape[0]
    block = rows * n
    wide = queries.shape[1] // n
    group = wide // HEAD
    blocks = 2 * FAR + 1
    bf16, f32 = jnp.bfloat16, jnp.float32
    vmem = pltpu.VMEM
    dma = pltpu.SemaphoreType.DMA
    any_spec = pl.BlockSpec(memory_space=pl.ANY)
    like_q = jax.ShapeDtypeStruct(queries.shape, bf16)
    like_k = jax.ShapeDtypeStruct(keys.shape, bf16)
    grad_q, near_k, near_v, far_k, far_v = pl.pallas_call(
        kernel,
        out_shape=[like_q] + [like_k] * 4,
        in_specs=[any_spec] * 4 + [pl.BlockSpec(memory_space=pltpu.SMEM)],
        out_specs=[any_spec] * 5,
        scratch_shapes=[
            vmem(queries.shape, bf16),
            vmem(keys.shape, bf16),
            vmem(values.shape, bf16),
            vmem(grad_out.shape, bf16),
            vmem((2, block, wide // 2), bf16),
            vmem((2, block, wide // 2), bf16),
            vmem((2 * FAR + 2, block, HEAD), bf16),
            vmem((2 * FAR + 2, block, HEAD), bf16),
            vmem((blocks * group, block, block), f32),
            vmem((blocks * group, block, block), f32),
            vmem((blocks * group, 1, block), f32),
            vmem((1, block), jnp.int32),
            vmem((group, HEAD, block), f32),
            vmem((block, wide), bf16),
            vmem((FAR + 1, 2, block, HEAD), f32),
            vmem((FAR + 1, 2, block, HEAD), bf16),
            vmem((FAR + 1, 2, block, HEAD), bf16),
            vmem((FAR + 1, 2, block, HEAD), bf16),
            vmem((FAR, 2, block, HEAD), bf16),
            dma((4,)),
            dma((6,)),
            dma((6,)),
            dma((FAR, 2, HALVES)),
            dma((FAR, 2, HALVES)),
            dma((FAR + 1, 2, HALVES)),
            dma((FAR + 1, 2, HALVES)),
            dma((FAR, 2, HALVES)),
            dma((FAR, 2, HALVES)),
            dma((FAR + 1, 2)),
            dma((FAR + 1, 2)),
            dma((5,)),
            dma((5,)),
        ],
        compiler_params=pltpu.CompilerParams(
            collective_id=0, has_side_effects=True, vmem_limit_bytes=60 * 2**20
        ),
    )(queries, keys, values, grad_out, doc_lengths)
    grad_k = (near_k.astype(f32) + far_k.astype(f32)) * HEAD ** -0.5
    grad_v = near_v.astype(f32) + far_v.astype(f32)
    return grad_q, grad_k.astype(bf16), grad_v.astype(bf16)


def solution(mesh):
    placed = P(("ctx", "tp"), None)
    return jax.shard_map(
        shards,
        mesh=mesh,
        in_specs=(placed,) * 4 + (P(),),
        out_specs=(placed,) * 3,
        check_vma=False,
    )
```

```python
import jax
import jax.numpy as jnp
from jax import lax
from jax.experimental import pallas as pl
from jax.experimental.pallas import tpu as pltpu
from jax.sharding import PartitionSpec as P

HEAD = 128
FAR = 4
HALVES = 2
MESH = pl.DeviceIdType.MESH
LOG2E = 1.4426950408889634
LOW = -1e30

NT = (((1,), (1,)), ((), ()))


def dot(a, b, dims=(((1,), (0,)), ((), ()))):
    return lax.dot_general(a, b, dims, preferred_element_type=jnp.float32)


def kernel(
    q_in, k_in, v_in, c_in, lengths,
    gq_out, near_out, far_out,
    qc_stage, kv_stage, qc_blk, kv_win, weights, dprobs, tops, starts,
    dq_acc, dq_out, own, sib_out, sib_in, back_out, back_in,
    stage_sem, in_send, in_recv, fwd_send, fwd_recv, pair_send, pair_recv,
    back_send, back_recv, term_send, term_recv, out_send, out_recv,
):
    n = lax.axis_size("tp")
    ring = lax.axis_size("ctx")
    me = lax.axis_index("ctx")
    y = lax.axis_index("tp")
    core = lax.rem(me, 2)
    chip = me // 2
    last = ring // 2 - 1
    after = lax.rem(me + 2, ring)
    before = lax.rem(me + ring - 2, ring)
    twin = me + 1 - 2 * core
    rows = q_in.shape[0]
    block = rows * n
    half = block // HALVES
    wide = qc_blk.shape[2]
    group = wide // HEAD
    factor = HEAD ** -0.5
    scale = factor * LOG2E
    mine = 1 - core
    offsets = sorted(range(1, n), key=lambda o: -min(o, n - o))

    barrier = pltpu.get_barrier_semaphore()
    for o in offsets:
        pl.semaphore_signal(
            barrier, inc=1, device_id=(me, lax.rem(y + o, n)), device_id_type=MESH
        )
    for other in (before, twin):
        pl.semaphore_signal(barrier, inc=1, device_id=(other, y), device_id_type=MESH)

    staged = (
        (k_in, kv_stage.at[0]),
        (v_in, kv_stage.at[1]),
        (q_in, qc_stage.at[0]),
        (c_in, qc_stage.at[1]),
    )
    for index, (src, dst) in enumerate(staged):
        pltpu.make_async_copy(src, dst, stage_sem.at[index]).start()

    position = me * block + lax.broadcasted_iota(jnp.int32, (1, block), 1)
    begin = jnp.zeros((1, block), jnp.int32)
    end = jnp.int32(0)
    for d in range(lengths.shape[0]):
        end = end + lengths[d]
        begin = jnp.where(position >= end, end, begin)
    starts[...] = begin
    key_row = lax.broadcasted_iota(jnp.int32, (block, block), 0)
    query_lane = lax.broadcasted_iota(jnp.int32, (block, block), 1)
    dq_acc[...] = jnp.zeros_like(dq_acc)

    for step in range(1, FAR + 1):
        @pl.when(chip < step)
        def _():
            kv_win[2 * step : 2 * step + 2] = jnp.zeros((2, *kv_win.shape[1:]), kv_win.dtype)

    @pl.when(chip == last)
    def _():
        back_in[...] = jnp.zeros_like(back_in)


    for index, (src, dst) in enumerate(staged):
        pltpu.make_async_copy(src, dst, stage_sem.at[index]).wait()
    pl.semaphore_wait(barrier, n + 1)

    here = pl.ds(pl.multiple_of(y * rows, rows), rows)

    def spread(index, src, width, dst):
        def of(p):
            return src.at[:, :, pl.ds(pl.multiple_of(p * width, width), width)]

        for o in offsets:
            to = lax.rem(y + o, n)
            pltpu.make_async_remote_copy(
                src_ref=of(to),
                dst_ref=dst,
                send_sem=in_send.at[index],
                recv_sem=in_recv.at[index],
                device_id=(me, to),
                device_id_type=MESH,
            ).start()
        pltpu.make_async_copy(of(y), dst, in_recv.at[index]).start()

    spread(0, kv_stage, HEAD, kv_win.at[mine, :, here, :])
    for h in range(group):
        for o in offsets + [0]:
            to = lax.rem(y + o, n)
            src = qc_stage.at[:, :, pl.ds(pl.multiple_of(to * wide + h * HEAD, HEAD), HEAD)]
            dst = qc_blk.at[:, here, h * HEAD : (h + 1) * HEAD]
            if o:
                pltpu.make_async_remote_copy(
                    src_ref=src, dst_ref=dst, send_sem=in_send.at[1], recv_sem=in_recv.at[1],
                    device_id=(me, to), device_id_type=MESH,
                ).start()
            else:
                pltpu.make_async_copy(src, dst, in_recv.at[1]).start()

    def got(ref, sem):
        pltpu.make_async_copy(ref, ref, sem).wait()

    pieces = [(index, part) for index in range(2) for part in range(HALVES)]

    def forward(piece, step):
        index, part = piece
        at = 2 * step + mine
        span = pl.ds(part * half, half)
        return pltpu.make_async_remote_copy(
            src_ref=kv_win.at[at, index, span],
            dst_ref=kv_win.at[at + 2, index, span],
            send_sem=fwd_send.at[step, index, part],
            recv_sem=fwd_recv.at[step, index, part],
            device_id=(after, y),
            device_id_type=MESH,
        )

    def share(piece, step):
        index, part = piece
        at = 2 * step + mine
        span = pl.ds(part * half, half)
        return pltpu.make_async_remote_copy(
            src_ref=kv_win.at[at, index, span],
            dst_ref=kv_win.at[at, index, span],
            send_sem=pair_send.at[step, index, part],
            recv_sem=pair_recv.at[step, index, part],
            device_id=(twin, y),
            device_id_type=MESH,
        )

    def relay(step):
        @pl.when(chip >= step)
        def _():
            for piece in pieces:
                forward(piece, step - 1).wait_recv()
                if step < FAR:
                    @pl.when(chip < last)
                    def _():
                        forward(piece, step).start()

                share(piece, step).start()

    def shared(step):
        @pl.when(chip >= step)
        def _():
            for piece in pieces:
                share(piece, step).wait_recv()

    def of_head(index, h):
        return qc_blk[index, :, h * HEAD : (h + 1) * HEAD]

    def scan_block(far, carry, diagonal=False):
        at = far + mine
        k = kv_win[at, 0]
        v = kv_win[at, 1]
        allowed = key_row >= starts[...] - (me - far) * block
        if diagonal:
            allowed = allowed & (key_row <= query_lane)
        new = []
        for h in range(group):
            s = dot(k, of_head(0, h), NT)
            dp = dot(v, of_head(1, h), NT)
            s = jnp.where(allowed, s, LOW)
            top = jnp.max(s, axis=0, keepdims=True)
            if not diagonal:
                top = jnp.maximum(top, carry[h][0])
            e = jnp.exp2(s * scale - top * scale)
            total = jnp.sum(e, axis=0, keepdims=True)
            weighted = jnp.sum(e * dp, axis=0, keepdims=True)
            if not diagonal:
                old, old_total, old_weighted = carry[h]
                shrink = jnp.exp2((old - top) * scale)
                total = total + old_total * shrink
                weighted = weighted + old_weighted * shrink
            weights[far * group + h] = e
            dprobs[far * group + h] = dp
            tops[far * group + h] = top
            new.append((top, total, weighted))
        return tuple(new)

    def scan(first, last, carry):
        return lax.fori_loop(first, last + 1, scan_block, carry)

    got(kv_win.at[mine], in_recv.at[0])

    @pl.when(chip < last)
    def _():
        for piece in pieces:
            forward(piece, 0).start()

    for piece in pieces:
        share(piece, 0).start()
    for step in range(1, FAR):
        relay(step)
    got(qc_blk, in_recv.at[1])
    stats = scan_block(0, None, True)
    for step in range(FAR):
        shared(step)
    stats = scan(1, 2 * FAR - 2, stats)
    relay(FAR)
    stats = scan_block(2 * FAR, stats)
    shared(FAR)
    stats = scan_block(2 * FAR - 1, stats)

    def terms(far):
        at = far + mine
        k_t = kv_win[at, 0].T
        dk = jnp.zeros((block, HEAD), jnp.float32)
        dv = jnp.zeros((block, HEAD), jnp.float32)
        for h in range(group):
            top, total, weighted = stats[h]
            inv = 1.0 / total
            shrink = jnp.exp2((tops[far * group + h] - top) * scale) * inv
            p = weights[far * group + h] * shrink
            ds = (p * (dprobs[far * group + h] - weighted * inv)).astype(jnp.bfloat16)
            dv = dv + dot(p.astype(jnp.bfloat16), of_head(1, h))
            dk = dk + dot(ds, of_head(0, h))
            dq_acc[h] += dot(k_t, ds)
        return dk, dv

    def hand_over(step):
        return pltpu.make_async_remote_copy(
            src_ref=sib_out.at[step],
            dst_ref=sib_in.at[step],
            send_sem=term_send.at[step],
            recv_sem=term_recv.at[step],
            device_id=(twin, y),
            device_id_type=MESH,
        )

    def back(piece, step):
        index, part = piece
        span = pl.ds(part * half, half)
        return pltpu.make_async_remote_copy(
            src_ref=back_out.at[step, index, span],
            dst_ref=back_in.at[step - 1, index, span],
            send_sem=back_send.at[step - 1, index, part],
            recv_sem=back_recv.at[step - 1, index, part],
            device_id=(before, y),
            device_id_type=MESH,
        )

    def gives(step):
        return (step >= 1 - core) & (step <= FAR - core)

    def takes(step):
        return (step >= core) & (step <= FAR - 1 + core)

    def make_terms(step):
        @pl.when(gives(step))
        def _():
            for index, term in enumerate(terms(2 * step - 1 + 2 * core)):
                sib_out[step, index] = term.astype(jnp.bfloat16)
            hand_over(step).start()

        for index, term in enumerate(terms(2 * step)):
            own[step, index] = term

    def take(step):
        @pl.when(takes(step))
        def _():
            hand_over(step).wait_recv()
            own[step] += sib_in[step].astype(jnp.float32)

    def pass_on(step):
        @pl.when(chip >= step)
        def _():
            for index, part in pieces:
                span = pl.ds(part * half, half)
                sums = own[step, index, span]
                if step < FAR:
                    @pl.when(chip < last)
                    def _():
                        back((index, part), step + 1).wait_recv()

                    sums = sums + back_in[step, index, span].astype(jnp.float32)
                back_out[step, index, span] = sums.astype(jnp.bfloat16)
                if step > 1:
                    back((index, part), step).start()

    def make_step(i, carry):
        step = FAR - i
        make_terms(step)

        @pl.when(step == FAR - 1)
        def _():
            take(FAR)
            pass_on(FAR)

        return carry

    def deliver(index, src, dst, to_ctx, others):
        def at(p):
            rows_of = pl.ds(pl.multiple_of(p * rows, rows), rows)
            return src.at[:, rows_of, :] if len(src.shape) == 3 else src.at[rows_of, :]

        for o in others:
            to = lax.rem(y + o, n)
            pltpu.make_async_remote_copy(
                src_ref=at(to),
                dst_ref=dst.at[y],
                send_sem=out_send.at[index],
                recv_sem=out_recv.at[index],
                device_id=(to_ctx, to),
                device_id_type=MESH,
            ).start()
        if 0 not in others:
            pltpu.make_async_copy(at(y), dst.at[y], out_recv.at[index]).start()

    lax.fori_loop(0, FAR + 1, make_step, 0)
    take(3)
    pass_on(3)
    for h in range(group):
        dq_out[:, h * HEAD : (h + 1) * HEAD] = (dq_acc[h] * factor).T.astype(jnp.bfloat16)
    deliver(0, dq_out, gq_out, me, offsets)
    take(0)
    back_out[0] = own[0].astype(jnp.bfloat16)
    deliver(1, back_out.at[0], near_out, me, offsets)
    take(2)
    pass_on(2)
    take(1)
    pass_on(1)

    @pl.when(chip > 0)
    def _():
        deliver(2, back_out.at[1], far_out, before, offsets + [0])

    @pl.when(chip == last)
    def _():
        for p in range(n):
            pltpu.make_async_copy(
                back_in.at[0, :, p * rows : (p + 1) * rows], far_out.at[p], out_recv.at[2]
            ).start()

    for index, ref in enumerate((gq_out, near_out, far_out)):
        got(ref, out_recv.at[index])

    got(kv_stage.at[:, :, pl.ds(0, (n - 1) * HEAD)], in_send.at[0])
    got(qc_stage.at[:, :, pl.ds(0, (n - 1) * wide)], in_send.at[1])
    got(dq_out.at[pl.ds(0, (n - 1) * rows), :], out_send.at[0])
    got(back_out.at[0, :, pl.ds(0, (n - 1) * rows), :], out_send.at[1])

    @pl.when(chip > 0)
    def _():
        got(back_out.at[1], out_send.at[2])

    for step in range(FAR + 1):
        @pl.when(chip >= step)
        def _():
            for piece in pieces:
                share(piece, step).wait_send()
                if step > 1:
                    back(piece, step).wait_send()

        if step < FAR:
            @pl.when((chip >= step) & (chip < last))
            def _():
                for piece in pieces:
                    forward(piece, step).wait_send()

    for step in range(FAR + 1):
        @pl.when(gives(step))
        def _():
            hand_over(step).wait_send()


def finish(gq_in, near_in, far_in, gq_out, gk_out, gv_out, gq_blk, parts, sums, sems):
    n, rows, wide = gq_in.shape

    def queries_of(p):
        return pltpu.make_async_copy(
            gq_in.at[p], gq_blk.at[:, p * wide : (p + 1) * wide], sems.at[0]
        )

    loads = [
        pltpu.make_async_copy(src, parts.at[i], sems.at[1 + i])
        for i, src in enumerate((near_in, far_in))
    ]
    for load in loads:
        load.start()
    for p in range(n):
        queries_of(p).start()
    for load in loads:
        load.wait()
    stores = []
    for index, (dst, factor) in enumerate(((gk_out, HEAD ** -0.5), (gv_out, 1.0))):
        for p in range(n):
            total = parts[0, p, index].astype(jnp.float32) + parts[1, p, index].astype(jnp.float32)
            sums[index, :, p * HEAD : (p + 1) * HEAD] = (total * factor).astype(jnp.bfloat16)
        stores.append(pltpu.make_async_copy(sums.at[index], dst, sems.at[3 + index]))
        stores[-1].start()
    pltpu.make_async_copy(gq_blk, gq_blk, sems.at[0]).wait()
    stores.append(pltpu.make_async_copy(gq_blk, gq_out, sems.at[5]))
    stores[-1].start()
    for store in stores:
        store.wait()


def shards(queries, keys, values, grad_out, doc_lengths):
    n = lax.axis_size("tp")
    rows = queries.shape[0]
    block = rows * n
    wide = queries.shape[1] // n
    group = wide // HEAD
    blocks = 2 * FAR + 1
    bf16, f32 = jnp.bfloat16, jnp.float32
    vmem = pltpu.VMEM
    dma = pltpu.SemaphoreType.DMA
    any_spec = pl.BlockSpec(memory_space=pl.ANY)
    like_q = jax.ShapeDtypeStruct(queries.shape, bf16)
    like_k = jax.ShapeDtypeStruct(keys.shape, bf16)
    split_q = jax.ShapeDtypeStruct((n, rows, wide), bf16)
    split_kv = jax.ShapeDtypeStruct((n, 2, rows, HEAD), bf16)
    parts = pl.pallas_call(
        kernel,
        out_shape=[split_q] + [split_kv] * 2,
        in_specs=[any_spec] * 4 + [pl.BlockSpec(memory_space=pltpu.SMEM)],
        out_specs=[any_spec] * 3,
        scratch_shapes=[
            vmem((2, *queries.shape), bf16),
            vmem((2, *keys.shape), bf16),
            vmem((2, block, wide), bf16),
            vmem((2 * FAR + 2, 2, block, HEAD), bf16),
            vmem((blocks * group, block, block), f32),
            vmem((blocks * group, block, block), f32),
            vmem((blocks * group, 1, block), f32),
            vmem((1, block), jnp.int32),
            vmem((group, HEAD, block), f32),
            vmem((block, wide), bf16),
            vmem((FAR + 1, 2, block, HEAD), f32),
            vmem((FAR + 1, 2, block, HEAD), bf16),
            vmem((FAR + 1, 2, block, HEAD), bf16),
            vmem((FAR + 1, 2, block, HEAD), bf16),
            vmem((FAR, 2, block, HEAD), bf16),
            dma((4,)),
            dma((2,)),
            dma((2,)),
            dma((FAR, 2, HALVES)),
            dma((FAR, 2, HALVES)),
            dma((FAR + 1, 2, HALVES)),
            dma((FAR + 1, 2, HALVES)),
            dma((FAR, 2, HALVES)),
            dma((FAR, 2, HALVES)),
            dma((FAR + 1,)),
            dma((FAR + 1,)),
            dma((3,)),
            dma((3,)),
        ],
        compiler_params=pltpu.CompilerParams(
            collective_id=0, has_side_effects=True, vmem_limit_bytes=60 * 2**20
        ),
    )(queries, keys, values, grad_out, doc_lengths)
    return pl.pallas_call(
        finish,
        out_shape=[like_q, like_k, like_k],
        in_specs=[any_spec] * 3,
        out_specs=[any_spec] * 3,
        scratch_shapes=[
            vmem(queries.shape, bf16),
            vmem((2, n, 2, rows, HEAD), bf16),
            vmem((2, *keys.shape), bf16),
            dma((6,)),
        ],
        compiler_params=pltpu.CompilerParams(vmem_limit_bytes=60 * 2**20),
    )(*parts)


def solution(mesh):
    placed = P(("ctx", "tp"), None)
    return jax.shard_map(
        shards,
        mesh=mesh,
        in_specs=(placed,) * 4 + (P(),),
        out_specs=(placed,) * 3,
        check_vma=False,
    )
```

```python
import functools

import jax
import jax.numpy as jnp
from jax import lax
from jax.experimental import pallas as pl
from jax.experimental.pallas import tpu as pltpu
from jax.sharding import PartitionSpec as P

HEAD = 128
FAR = 4
HALVES = 2
MESH = pl.DeviceIdType.MESH
LOG2E = 1.4426950408889634
LOW = -1e30

NT = (((1,), (1,)), ((), ()))


def dot(a, b, dims=(((1,), (0,)), ((), ()))):
    return lax.dot_general(a, b, dims, preferred_element_type=jnp.float32)


def kernel(
    q_in, k_in, v_in, c_in, lengths,
    gq_out, near_out, far_out,
    qc_stage, kv_stage, qc_blk, kv_win, weights, dprobs, tops, starts,
    dq_acc, dq_out, own, sib_out, sib_in, back_out, back_in,
    stage_sem, home_sem, in_send, in_recv, fwd_send, fwd_recv, pair_send, pair_recv,
    back_send, back_recv, term_send, term_recv, out_send, out_recv,
):
    n = lax.axis_size("tp")
    ring = lax.axis_size("ctx")
    me = lax.axis_index("ctx")
    y = lax.axis_index("tp")
    core = lax.rem(me, 2)
    chip = me // 2
    last = ring // 2 - 1
    after = lax.rem(me + 2, ring)
    before = lax.rem(me + ring - 2, ring)
    twin = me + 1 - 2 * core
    rows = q_in.shape[0]
    block = rows * n
    half = block // HALVES
    wide = qc_blk.shape[2]
    group = wide // HEAD
    factor = HEAD ** -0.5
    scale = factor * LOG2E
    mine = 1 - core
    offsets = sorted(range(1, n), key=lambda o: -min(o, n - o))

    barrier = pltpu.get_barrier_semaphore()
    for o in offsets:
        pl.semaphore_signal(
            barrier, inc=1, device_id=(me, lax.rem(y + o, n)), device_id_type=MESH
        )
        pl.semaphore_signal(
            barrier, inc=1, device_id=(before, lax.rem(y + o, n)), device_id_type=MESH
        )
    for other in (before, twin):
        pl.semaphore_signal(barrier, inc=1, device_id=(other, y), device_id_type=MESH)

    staged = (
        (k_in, kv_stage.at[0]),
        (v_in, kv_stage.at[1]),
        (q_in, qc_stage.at[0]),
        (c_in, qc_stage.at[1]),
    )
    for index, (src, dst) in enumerate(staged):
        pltpu.make_async_copy(src, dst, stage_sem.at[index]).start()

    position = me * block + lax.broadcasted_iota(jnp.int32, (1, block), 1)
    begin = jnp.zeros((1, block), jnp.int32)
    end = jnp.int32(0)
    for d in range(lengths.shape[0]):
        end = end + lengths[d]
        begin = jnp.where(position >= end, end, begin)
    starts[...] = begin
    key_row = lax.broadcasted_iota(jnp.int32, (block, block), 0)
    query_lane = lax.broadcasted_iota(jnp.int32, (block, block), 1)
    dq_acc[...] = jnp.zeros_like(dq_acc)

    for step in range(1, FAR + 1):
        @pl.when(chip < step)
        def _():
            kv_win[2 * step : 2 * step + 2] = jnp.zeros((2, *kv_win.shape[1:]), kv_win.dtype)

    @pl.when(chip == last)
    def _():
        back_in[...] = jnp.zeros_like(back_in)


    for index, (src, dst) in enumerate(staged):
        pltpu.make_async_copy(src, dst, stage_sem.at[index]).wait()
    pl.semaphore_wait(barrier, 2 * n)

    here = pl.ds(pl.multiple_of(y * rows, rows), rows)

    def spread(index, src, width, dst, to_ctx, others):
        def of(p):
            return src.at[:, :, pl.ds(pl.multiple_of(p * width, width), width)]

        for o in others:
            to = lax.rem(y + o, n)
            pltpu.make_async_remote_copy(
                src_ref=of(to),
                dst_ref=dst,
                send_sem=in_send.at[index],
                recv_sem=in_recv.at[index],
                device_id=(to_ctx, to),
                device_id_type=MESH,
            ).start()
        if 0 not in others:
            pltpu.make_async_copy(of(y), dst, in_recv.at[index]).start()

    @pl.when(chip < last)
    def _():
        spread(2, kv_stage, HEAD, kv_win.at[mine + 2, :, here, :], after, offsets + [0])

    @pl.when(chip == last)
    def _():
        spread(0, kv_stage, HEAD, kv_win.at[mine, :, here, :], me, offsets)

    def side_sem(h):
        return 1 if h < group // 2 else 3

    for h in range(group):
        for o in offsets + [0]:
            to = lax.rem(y + o, n)
            src = qc_stage.at[:, :, pl.ds(pl.multiple_of(to * wide + h * HEAD, HEAD), HEAD)]
            dst = qc_blk.at[:, here, h * HEAD : (h + 1) * HEAD]
            if o:
                pltpu.make_async_remote_copy(
                    src_ref=src,
                    dst_ref=dst,
                    send_sem=in_send.at[side_sem(h)],
                    recv_sem=in_recv.at[side_sem(h)],
                    device_id=(me, to),
                    device_id_type=MESH,
                ).start()
            else:
                pltpu.make_async_copy(src, dst, in_recv.at[side_sem(h)]).start()

    def got(ref, sem):
        pltpu.make_async_copy(ref, ref, sem).wait()

    pieces = [(index, part) for index in range(2) for part in range(HALVES)]

    def forward(piece, step):
        index, part = piece
        at = 2 * step + mine
        span = pl.ds(part * half, half)
        return pltpu.make_async_remote_copy(
            src_ref=kv_win.at[at, index, span],
            dst_ref=kv_win.at[at + 2, index, span],
            send_sem=fwd_send.at[step, index, part],
            recv_sem=fwd_recv.at[step, index, part],
            device_id=(after, y),
            device_id_type=MESH,
        )

    def share(piece, step):
        index, part = piece
        at = 2 * step + mine
        span = pl.ds(part * half, half)
        return pltpu.make_async_remote_copy(
            src_ref=kv_win.at[at, index, span],
            dst_ref=kv_win.at[at, index, span],
            send_sem=pair_send.at[step, index, part],
            recv_sem=pair_recv.at[step, index, part],
            device_id=(twin, y),
            device_id_type=MESH,
        )

    def relay(step):
        @pl.when(chip >= step)
        def _():
            if step == 1:
                got(kv_win.at[mine + 2], in_recv.at[2])
            for piece in pieces:
                if step > 1:
                    forward(piece, step - 1).wait_recv()
                if step < FAR:
                    @pl.when(chip < last)
                    def _():
                        forward(piece, step).start()

                share(piece, step).start()

    def give_back():
        return pltpu.make_async_remote_copy(
            src_ref=kv_win.at[mine + 2],
            dst_ref=kv_win.at[mine],
            send_sem=home_sem.at[0],
            recv_sem=home_sem.at[1],
            device_id=(before, y),
            device_id_type=MESH,
        )

    def shared(step):
        @pl.when(chip >= step)
        def _():
            for piece in pieces:
                share(piece, step).wait_recv()

    def of_head(index, h):
        return qc_blk[index, :, h * HEAD : (h + 1) * HEAD]

    def scan_blocks(fars, heads, carry, diagonal=False):
        allowed = []
        for far in fars:
            inside = key_row >= starts[...] - (me - far) * block
            allowed.append(inside & (key_row <= query_lane) if diagonal else inside)
        new = []
        for j, h in enumerate(heads):
            scores = []
            for far, inside in zip(fars, allowed):
                s = dot(kv_win[far + mine, 0], of_head(0, h), NT)
                scores.append(jnp.where(inside, s, LOW))
            tops_here = [jnp.max(s, axis=0, keepdims=True) for s in scores]
            if not diagonal:
                tops_here.append(carry[j][0])
            top = functools.reduce(jnp.maximum, tops_here)
            total = jnp.zeros((1, block), jnp.float32)
            weighted = jnp.zeros((1, block), jnp.float32)
            if not diagonal:
                old, total, weighted = carry[j]
                shrink = jnp.exp2((old - top) * scale)
                total = total * shrink
                weighted = weighted * shrink
            for far, s in zip(fars, scores):
                dp = dot(kv_win[far + mine, 1], of_head(1, h), NT)
                e = jnp.exp2(s * scale - top * scale)
                total = total + jnp.sum(e, axis=0, keepdims=True)
                weighted = weighted + jnp.sum(e * dp, axis=0, keepdims=True)
                weights[far * group + h] = e
                dprobs[far * group + h] = dp
                tops[far * group + h] = top
            new.append((top, total, weighted))
        return tuple(new)

    def scan_side(heads):
        carry = scan_blocks((0,), heads, None, True)
        return lax.fori_loop(
            0, FAR - 1, lambda i, c: scan_blocks((2 * i + 1, 2 * i + 2), heads, c), carry
        )

    relay(1)

    @pl.when(chip > 0)
    def _():
        give_back().start()

    relay(2)

    @pl.when(chip < last)
    def _():
        give_back().wait_recv()

    @pl.when(chip == last)
    def _():
        got(kv_win.at[mine], in_recv.at[0])

    for piece in pieces:
        share(piece, 0).start()
    relay(3)
    for step in range(FAR):
        shared(step)
    stats = ()
    for side in range(2):
        heads = tuple(range(side * group // 2, (side + 1) * group // 2))
        sem = in_recv.at[side_sem(heads[0])]
        got(qc_blk.at[:, :, heads[0] * HEAD : (heads[-1] + 1) * HEAD], sem)
        stats += scan_side(heads)
    relay(FAR)
    stats = scan_blocks((2 * FAR,), range(group), stats)
    shared(FAR)
    stats = scan_blocks((2 * FAR - 1,), range(group), stats)

    def terms(far):
        at = far + mine
        k_t = kv_win[at, 0].T
        dk = jnp.zeros((block, HEAD), jnp.float32)
        dv = jnp.zeros((block, HEAD), jnp.float32)
        for h in range(group):
            top, total, weighted = stats[h]
            inv = 1.0 / total
            shrink = jnp.exp2((tops[far * group + h] - top) * scale) * inv
            p = weights[far * group + h] * shrink
            ds = (p * (dprobs[far * group + h] - weighted * inv)).astype(jnp.bfloat16)
            dv = dv + dot(p.astype(jnp.bfloat16), of_head(1, h))
            dk = dk + dot(ds, of_head(0, h))
            dq_acc[h] += dot(k_t, ds)
        return dk, dv

    def hand_over(step):
        return pltpu.make_async_remote_copy(
            src_ref=sib_out.at[step],
            dst_ref=sib_in.at[step],
            send_sem=term_send.at[step],
            recv_sem=term_recv.at[step],
            device_id=(twin, y),
            device_id_type=MESH,
        )

    def back(piece, step):
        index, part = piece
        span = pl.ds(part * half, half)
        return pltpu.make_async_remote_copy(
            src_ref=back_out.at[step, index, span],
            dst_ref=back_in.at[step - 1, index, span],
            send_sem=back_send.at[step - 1, index, part],
            recv_sem=back_recv.at[step - 1, index, part],
            device_id=(before, y),
            device_id_type=MESH,
        )

    def gives(step):
        return (step >= 1 - core) & (step <= FAR - core)

    def takes(step):
        return (step >= core) & (step <= FAR - 1 + core)

    def make_terms(step):
        @pl.when(gives(step))
        def _():
            for index, term in enumerate(terms(2 * step - 1 + 2 * core)):
                sib_out[step, index] = term.astype(jnp.bfloat16)
            hand_over(step).start()

        for index, term in enumerate(terms(2 * step)):
            own[step, index] = term

    def take(step):
        @pl.when(takes(step))
        def _():
            hand_over(step).wait_recv()
            own[step] += sib_in[step].astype(jnp.float32)

    def pass_on(step):
        @pl.when(chip >= step)
        def _():
            for index, part in pieces:
                span = pl.ds(part * half, half)
                sums = own[step, index, span]
                if step < FAR:
                    @pl.when(chip < last)
                    def _():
                        back((index, part), step + 1).wait_recv()

                    sums = sums + back_in[step, index, span].astype(jnp.float32)
                back_out[step, index, span] = sums.astype(jnp.bfloat16)
                if step > 1:
                    back((index, part), step).start()

    def make_step(i, carry):
        step = FAR - i
        make_terms(step)

        @pl.when(step == FAR - 1)
        def _():
            take(FAR)
            pass_on(FAR)

        return carry

    def deliver(index, src, dst, to_ctx, others):
        def at(p):
            rows_of = pl.ds(pl.multiple_of(p * rows, rows), rows)
            return src.at[:, rows_of, :] if len(src.shape) == 3 else src.at[rows_of, :]

        for o in others:
            to = lax.rem(y + o, n)
            pltpu.make_async_remote_copy(
                src_ref=at(to),
                dst_ref=dst.at[y],
                send_sem=out_send.at[index],
                recv_sem=out_recv.at[index],
                device_id=(to_ctx, to),
                device_id_type=MESH,
            ).start()
        if 0 not in others:
            pltpu.make_async_copy(at(y), dst.at[y], out_recv.at[index]).start()

    lax.fori_loop(0, FAR + 1, make_step, 0)
    take(3)
    pass_on(3)
    for h in range(group):
        dq_out[:, h * HEAD : (h + 1) * HEAD] = (dq_acc[h] * factor).T.astype(jnp.bfloat16)
    deliver(0, dq_out, gq_out, me, offsets)
    take(0)
    back_out[0] = own[0].astype(jnp.bfloat16)
    deliver(1, back_out.at[0], near_out, me, offsets)
    take(2)
    pass_on(2)
    take(1)
    pass_on(1)

    @pl.when(chip > 0)
    def _():
        deliver(2, back_out.at[1], far_out, before, offsets + [0])

    @pl.when(chip == last)
    def _():
        for p in range(n):
            pltpu.make_async_copy(
                back_in.at[0, :, p * rows : (p + 1) * rows], far_out.at[p], out_recv.at[2]
            ).start()

    for index, ref in enumerate((gq_out, near_out, far_out)):
        got(ref, out_recv.at[index])

    @pl.when(chip == last)
    def _():
        got(kv_stage.at[:, :, pl.ds(0, (n - 1) * HEAD)], in_send.at[0])

    @pl.when(chip > 0)
    def _():
        give_back().wait_send()

    @pl.when(chip < last)
    def _():
        got(kv_stage, in_send.at[2])

    for index in (1, 3):
        got(qc_stage.at[:, :, pl.ds(0, (n - 1) * wide // 2)], in_send.at[index])
    got(dq_out.at[pl.ds(0, (n - 1) * rows), :], out_send.at[0])
    got(back_out.at[0, :, pl.ds(0, (n - 1) * rows), :], out_send.at[1])

    @pl.when(chip > 0)
    def _():
        got(back_out.at[1], out_send.at[2])

    for step in range(FAR + 1):
        @pl.when(chip >= step)
        def _():
            for piece in pieces:
                share(piece, step).wait_send()
                if step > 1:
                    back(piece, step).wait_send()

        if 0 < step < FAR:
            @pl.when((chip >= step) & (chip < last))
            def _():
                for piece in pieces:
                    forward(piece, step).wait_send()

    for step in range(FAR + 1):
        @pl.when(gives(step))
        def _():
            hand_over(step).wait_send()


def finish(gq_in, near_in, far_in, gq_out, gk_out, gv_out, gq_blk, parts, sums, sems):
    n, rows, wide = gq_in.shape

    def queries_of(p):
        return pltpu.make_async_copy(
            gq_in.at[p], gq_blk.at[:, p * wide : (p + 1) * wide], sems.at[0]
        )

    loads = [
        pltpu.make_async_copy(src, parts.at[i], sems.at[1 + i])
        for i, src in enumerate((near_in, far_in))
    ]
    for load in loads:
        load.start()
    for p in range(n):
        queries_of(p).start()
    for load in loads:
        load.wait()
    stores = []
    for index, (dst, factor) in enumerate(((gk_out, HEAD ** -0.5), (gv_out, 1.0))):
        for p in range(n):
            total = parts[0, p, index].astype(jnp.float32) + parts[1, p, index].astype(jnp.float32)
            sums[index, :, p * HEAD : (p + 1) * HEAD] = (total * factor).astype(jnp.bfloat16)
        stores.append(pltpu.make_async_copy(sums.at[index], dst, sems.at[3 + index]))
        stores[-1].start()
    pltpu.make_async_copy(gq_blk, gq_blk, sems.at[0]).wait()
    stores.append(pltpu.make_async_copy(gq_blk, gq_out, sems.at[5]))
    stores[-1].start()
    for store in stores:
        store.wait()


def shards(queries, keys, values, grad_out, doc_lengths):
    n = lax.axis_size("tp")
    rows = queries.shape[0]
    block = rows * n
    wide = queries.shape[1] // n
    group = wide // HEAD
    blocks = 2 * FAR + 1
    bf16, f32 = jnp.bfloat16, jnp.float32
    vmem = pltpu.VMEM
    dma = pltpu.SemaphoreType.DMA
    any_spec = pl.BlockSpec(memory_space=pl.ANY)
    like_q = jax.ShapeDtypeStruct(queries.shape, bf16)
    like_k = jax.ShapeDtypeStruct(keys.shape, bf16)
    split_q = jax.ShapeDtypeStruct((n, rows, wide), bf16)
    split_kv = jax.ShapeDtypeStruct((n, 2, rows, HEAD), bf16)
    parts = pl.pallas_call(
        kernel,
        out_shape=[split_q] + [split_kv] * 2,
        in_specs=[any_spec] * 4 + [pl.BlockSpec(memory_space=pltpu.SMEM)],
        out_specs=[any_spec] * 3,
        scratch_shapes=[
            vmem((2, *queries.shape), bf16),
            vmem((2, *keys.shape), bf16),
            vmem((2, block, wide), bf16),
            vmem((2 * FAR + 2, 2, block, HEAD), bf16),
            vmem((blocks * group, block, block), f32),
            vmem((blocks * group, block, block), f32),
            vmem((blocks * group, 1, block), f32),
            vmem((1, block), jnp.int32),
            vmem((group, HEAD, block), f32),
            vmem((block, wide), bf16),
            vmem((FAR + 1, 2, block, HEAD), f32),
            vmem((FAR + 1, 2, block, HEAD), bf16),
            vmem((FAR + 1, 2, block, HEAD), bf16),
            vmem((FAR + 1, 2, block, HEAD), bf16),
            vmem((FAR, 2, block, HEAD), bf16),
            dma((4,)),
            dma((2,)),
            dma((4,)),
            dma((4,)),
            dma((FAR, 2, HALVES)),
            dma((FAR, 2, HALVES)),
            dma((FAR + 1, 2, HALVES)),
            dma((FAR + 1, 2, HALVES)),
            dma((FAR, 2, HALVES)),
            dma((FAR, 2, HALVES)),
            dma((FAR + 1,)),
            dma((FAR + 1,)),
            dma((3,)),
            dma((3,)),
        ],
        compiler_params=pltpu.CompilerParams(
            collective_id=0, has_side_effects=True, vmem_limit_bytes=60 * 2**20
        ),
    )(queries, keys, values, grad_out, doc_lengths)
    return pl.pallas_call(
        finish,
        out_shape=[like_q, like_k, like_k],
        in_specs=[any_spec] * 3,
        out_specs=[any_spec] * 3,
        scratch_shapes=[
            vmem(queries.shape, bf16),
            vmem((2, n, 2, rows, HEAD), bf16),
            vmem((2, *keys.shape), bf16),
            dma((6,)),
        ],
        compiler_params=pltpu.CompilerParams(vmem_limit_bytes=60 * 2**20),
    )(*parts)


def solution(mesh):
    placed = P(("ctx", "tp"), None)
    return jax.shard_map(
        shards,
        mesh=mesh,
        in_specs=(placed,) * 4 + (P(),),
        out_specs=(placed,) * 3,
        check_vma=False,
    )
```

```python
import functools

import jax
import jax.numpy as jnp
from jax import lax
from jax.experimental import pallas as pl
from jax.experimental.pallas import tpu as pltpu
from jax.sharding import PartitionSpec as P

HEAD = 128
FAR = 4
HALVES = 2
MESH = pl.DeviceIdType.MESH
LOG2E = 1.4426950408889634
LOW = -1e30

NT = (((1,), (1,)), ((), ()))


def dot(a, b, dims=(((1,), (0,)), ((), ()))):
    return lax.dot_general(a, b, dims, preferred_element_type=jnp.float32)


def kernel(
    q_in, k_in, v_in, c_in, lengths,
    gq_out, gkv_out,
    qc_stage, kv_stage, qc_blk, kv_win, weights, dprobs, tops, starts,
    dq_acc, dq_out, own, sib_acc, sib_out, sib_in, back_out, back_in, ahead_in,
    stage_sem, home_sem, in_send, in_recv, fwd_send, fwd_recv, pair_send, pair_recv,
    back_send, back_recv, ahead_send, ahead_recv, term_send, term_recv, out_send, out_recv,
):
    n = lax.axis_size("tp")
    ring = lax.axis_size("ctx")
    me = lax.axis_index("ctx")
    y = lax.axis_index("tp")
    core = lax.rem(me, 2)
    chip = me // 2
    last = ring // 2 - 1
    after = lax.rem(me + 2, ring)
    before = lax.rem(me + ring - 2, ring)
    source = lax.rem(me + ring - 4, ring)
    twin = me + 1 - 2 * core
    rows = q_in.shape[0]
    block = rows * n
    half = block // HALVES
    wide = qc_blk.shape[2]
    group = wide // HEAD
    factor = HEAD ** -0.5
    scale = factor * LOG2E
    mine = 1 - core
    offsets = sorted(range(1, n), key=lambda o: -min(o, n - o))

    barrier = pltpu.get_barrier_semaphore()
    for o in offsets:
        pl.semaphore_signal(
            barrier, inc=1, device_id=(me, lax.rem(y + o, n)), device_id_type=MESH
        )
        pl.semaphore_signal(
            barrier, inc=1, device_id=(before, lax.rem(y + o, n)), device_id_type=MESH
        )
    for other in (before, twin):
        pl.semaphore_signal(barrier, inc=1, device_id=(other, y), device_id_type=MESH)

    staged = (
        (k_in, kv_stage.at[0]),
        (v_in, kv_stage.at[1]),
        (q_in, qc_stage.at[0]),
        (c_in, qc_stage.at[1]),
    )
    for index, (src, dst) in enumerate(staged):
        pltpu.make_async_copy(src, dst, stage_sem.at[index]).start()

    position = me * block + lax.broadcasted_iota(jnp.int32, (1, block), 1)
    begin = jnp.zeros((1, block), jnp.int32)
    end = jnp.int32(0)
    for d in range(lengths.shape[0]):
        end = end + lengths[d]
        begin = jnp.where(position >= end, end, begin)
    starts[...] = begin
    key_row = lax.broadcasted_iota(jnp.int32, (block, block), 0)
    query_lane = lax.broadcasted_iota(jnp.int32, (block, block), 1)
    dq_acc[...] = jnp.zeros_like(dq_acc)

    for step in range(1, FAR + 1):
        @pl.when(chip < step)
        def _():
            kv_win[2 * step : 2 * step + 2] = jnp.zeros((2, *kv_win.shape[1:]), kv_win.dtype)

    @pl.when(chip == last)
    def _():
        back_in[...] = jnp.zeros_like(back_in)


    for index, (src, dst) in enumerate(staged):
        pltpu.make_async_copy(src, dst, stage_sem.at[index]).wait()
    pl.semaphore_wait(barrier, 2 * n)

    here = pl.ds(pl.multiple_of(y * rows, rows), rows)

    def spread(index, src, width, dst, to_ctx, others):
        def of(p):
            return src.at[:, :, pl.ds(pl.multiple_of(p * width, width), width)]

        for o in others:
            to = lax.rem(y + o, n)
            pltpu.make_async_remote_copy(
                src_ref=of(to),
                dst_ref=dst,
                send_sem=in_send.at[index],
                recv_sem=in_recv.at[index],
                device_id=(to_ctx, to),
                device_id_type=MESH,
            ).start()
        if 0 not in others:
            pltpu.make_async_copy(of(y), dst, in_recv.at[index]).start()

    @pl.when(chip < last)
    def _():
        spread(2, kv_stage, HEAD, kv_win.at[mine + 2, :, here, :], after, offsets + [0])

    @pl.when(chip == last)
    def _():
        spread(0, kv_stage, HEAD, kv_win.at[mine, :, here, :], me, offsets)

    def side_sem(h):
        return 1 if h < group // 2 else 3

    for h in range(group):
        for o in offsets + [0]:
            to = lax.rem(y + o, n)
            src = qc_stage.at[:, :, pl.ds(pl.multiple_of(to * wide + h * HEAD, HEAD), HEAD)]
            dst = qc_blk.at[:, here, h * HEAD : (h + 1) * HEAD]
            if o:
                pltpu.make_async_remote_copy(
                    src_ref=src,
                    dst_ref=dst,
                    send_sem=in_send.at[side_sem(h)],
                    recv_sem=in_recv.at[side_sem(h)],
                    device_id=(me, to),
                    device_id_type=MESH,
                ).start()
            else:
                pltpu.make_async_copy(src, dst, in_recv.at[side_sem(h)]).start()

    def got(ref, sem):
        pltpu.make_async_copy(ref, ref, sem).wait()

    pieces = [(index, part) for index in range(2) for part in range(HALVES)]

    def forward(piece, step):
        index, part = piece
        at = 2 * step + mine
        span = pl.ds(part * half, half)
        return pltpu.make_async_remote_copy(
            src_ref=kv_win.at[at, index, span],
            dst_ref=kv_win.at[at + 2, index, span],
            send_sem=fwd_send.at[step, index, part],
            recv_sem=fwd_recv.at[step, index, part],
            device_id=(after, y),
            device_id_type=MESH,
        )

    def share(piece, step):
        index, part = piece
        at = 2 * step + mine
        span = pl.ds(part * half, half)
        return pltpu.make_async_remote_copy(
            src_ref=kv_win.at[at, index, span],
            dst_ref=kv_win.at[at, index, span],
            send_sem=pair_send.at[step, index, part],
            recv_sem=pair_recv.at[step, index, part],
            device_id=(twin, y),
            device_id_type=MESH,
        )

    def relay(step):
        @pl.when(chip >= step)
        def _():
            if step == 1:
                got(kv_win.at[mine + 2], in_recv.at[2])
            for piece in pieces:
                if step > 1:
                    forward(piece, step - 1).wait_recv()
                if step < FAR:
                    @pl.when(chip < last)
                    def _():
                        forward(piece, step).start()

                share(piece, step).start()

    def give_back():
        return pltpu.make_async_remote_copy(
            src_ref=kv_win.at[mine + 2],
            dst_ref=kv_win.at[mine],
            send_sem=home_sem.at[0],
            recv_sem=home_sem.at[1],
            device_id=(before, y),
            device_id_type=MESH,
        )

    def shared(step):
        @pl.when(chip >= step)
        def _():
            for piece in pieces:
                share(piece, step).wait_recv()

    def of_head(index, h):
        return qc_blk[index, :, h * HEAD : (h + 1) * HEAD]

    def scan_blocks(fars, heads, carry, diagonal=False):
        allowed = []
        for far in fars:
            inside = key_row >= starts[...] - (me - far) * block
            allowed.append(inside & (key_row <= query_lane) if diagonal else inside)
        new = []
        for j, h in enumerate(heads):
            scores = []
            for far, inside in zip(fars, allowed):
                s = dot(kv_win[far + mine, 0], of_head(0, h), NT)
                scores.append(jnp.where(inside, s, LOW))
            tops_here = [jnp.max(s, axis=0, keepdims=True) for s in scores]
            if not diagonal:
                tops_here.append(carry[j][0])
            top = functools.reduce(jnp.maximum, tops_here)
            total = jnp.zeros((1, block), jnp.float32)
            weighted = jnp.zeros((1, block), jnp.float32)
            if not diagonal:
                old, total, weighted = carry[j]
                shrink = jnp.exp2((old - top) * scale)
                total = total * shrink
                weighted = weighted * shrink
            for far, s in zip(fars, scores):
                dp = dot(kv_win[far + mine, 1], of_head(1, h), NT)
                e = jnp.exp2(s * scale - top * scale)
                total = total + jnp.sum(e, axis=0, keepdims=True)
                weighted = weighted + jnp.sum(e * dp, axis=0, keepdims=True)
                weights[far * group + h] = e
                dprobs[far * group + h] = dp
                tops[far * group + h] = top
            new.append((top, total, weighted))
        return tuple(new)

    def scan_side(heads):
        carry = scan_blocks((0,), heads, None, True)
        return lax.fori_loop(
            0, FAR - 1, lambda i, c: scan_blocks((2 * i + 1, 2 * i + 2), heads, c), carry
        )

    relay(1)

    @pl.when(chip > 0)
    def _():
        give_back().start()

    relay(2)

    @pl.when(chip < last)
    def _():
        give_back().wait_recv()

    @pl.when(chip == last)
    def _():
        got(kv_win.at[mine], in_recv.at[0])

    for piece in pieces:
        share(piece, 0).start()
    relay(3)
    for step in range(FAR):
        shared(step)
    stats = ()
    sides = [tuple(range(i * group // 2, (i + 1) * group // 2)) for i in range(2)]
    for heads in sides:
        sem = in_recv.at[side_sem(heads[0])]
        got(qc_blk.at[:, :, heads[0] * HEAD : (heads[-1] + 1) * HEAD], sem)
        stats += scan_side(heads)
    relay(FAR)
    stats = scan_blocks((2 * FAR,), range(group), stats)
    shared(FAR)
    stats = scan_blocks((2 * FAR - 1,), range(group), stats)

    def terms(far, heads):
        at = far + mine
        k_t = kv_win[at, 0].T
        dk = jnp.zeros((block, HEAD), jnp.float32)
        dv = jnp.zeros((block, HEAD), jnp.float32)
        for h in heads:
            top, total, weighted = stats[h]
            inv = 1.0 / total
            shrink = jnp.exp2((tops[far * group + h] - top) * scale) * inv
            p = weights[far * group + h] * shrink
            ds = (p * (dprobs[far * group + h] - weighted * inv)).astype(jnp.bfloat16)
            dv = dv + dot(p.astype(jnp.bfloat16), of_head(1, h))
            dk = dk + dot(ds, of_head(0, h))
            dq_acc[h] += dot(k_t, ds)
        return dk, dv

    def hand_over(step):
        return pltpu.make_async_remote_copy(
            src_ref=sib_out.at[step],
            dst_ref=sib_in.at[step],
            send_sem=term_send.at[step],
            recv_sem=term_recv.at[step],
            device_id=(twin, y),
            device_id_type=MESH,
        )

    def back(piece, step):
        index, part = piece
        span = pl.ds(part * half, half)
        return pltpu.make_async_remote_copy(
            src_ref=back_out.at[step, index, span],
            dst_ref=back_in.at[step - 1, index, span],
            send_sem=back_send.at[step - 1, index, part],
            recv_sem=back_recv.at[step - 1, index, part],
            device_id=(before, y),
            device_id_type=MESH,
        )

    def gives(step):
        return (step >= 1 - core) & (step <= FAR - core)

    def takes(step):
        return (step >= core) & (step <= FAR - 1 + core)

    def make_terms(step):
        @pl.when(gives(step))
        def _():
            for index, term in enumerate(terms(2 * step - 1 + 2 * core, range(group))):
                sib_out[step, index] = term.astype(jnp.bfloat16)
            hand_over(step).start()

        for index, term in enumerate(terms(2 * step, range(group))):
            own[step, index] = term

    def take(step):
        @pl.when(takes(step))
        def _():
            hand_over(step).wait_recv()
            own[step] += sib_in[step].astype(jnp.float32)

    def ahead(piece, step):
        index, part = piece
        span = pl.ds(part * half, half)
        return pltpu.make_async_remote_copy(
            src_ref=back_out.at[step, index, span],
            dst_ref=ahead_in.at[step, index, span],
            send_sem=ahead_send.at[step, index, part],
            recv_sem=ahead_recv.at[step, index, part],
            device_id=(after, y),
            device_id_type=MESH,
        )

    def added(piece, step, *more):
        index, part = piece
        span = pl.ds(part * half, half)
        sums = own[step, index, span]
        for ref in more:
            sums = sums + ref[index, span].astype(jnp.float32)
        if step in (0, 2) and index == 0:
            sums = sums * factor
        back_out[step, index, span] = sums.astype(jnp.bfloat16)

    def pass_on(step):
        @pl.when(chip >= step)
        def _():
            for piece in pieces:
                if step < FAR:
                    @pl.when(chip < last)
                    def _():
                        back(piece, step + 1).wait_recv()

                    added(piece, step, back_in.at[step])
                else:
                    added(piece, step)
                back(piece, step).start()

    def pass_ahead_0():
        @pl.when(chip < last - 1)
        def _():
            for index, part in pieces:
                span = pl.ds(part * half, half)
                back_out[0, index, span] = own[0, index, span].astype(jnp.bfloat16)
                ahead((index, part), 0).start()

    def pass_ahead_1():
        @pl.when((chip >= 1) & (chip < last))
        def _():
            for piece in pieces:
                ahead(piece, 0).wait_recv()
                added(piece, 1, ahead_in.at[0])
                ahead(piece, 1).start()

        @pl.when(chip == last)
        def _():
            for piece in pieces:
                added(piece, 1)
                back(piece, 1).start()

    def make_step(i, carry):
        make_terms(FAR * (1 - i))
        return carry

    def make_side(side):
        heads = sides[side]

        def step_of(i, carry):
            step = jnp.where(i == 0, 3, i)
            other = terms(2 * step - 1 + 2 * core, heads)
            same = terms(2 * step, heads)
            for index in range(2):
                if side == 0:
                    sib_acc[step, index] = other[index]
                    own[step, index] = same[index]
                else:
                    sib_out[step, index] = (sib_acc[step, index] + other[index]).astype(jnp.bfloat16)
                    own[step, index] += same[index]
            if side == 1:
                hand_over(step).start()
            return carry

        lax.fori_loop(0, 3, step_of, 0)
        for h in heads:
            dq_out[side, :, (h - heads[0]) * HEAD : (h - heads[0] + 1) * HEAD] = (
                (dq_acc[h] * factor).T.astype(jnp.bfloat16)
            )

    def deliver(index, src, dst, to_ctx, others, side=None):
        def at(p):
            rows_of = pl.ds(pl.multiple_of(p * rows, rows), rows)
            return src.at[:, rows_of, :] if len(src.shape) == 3 else src.at[rows_of, :]

        there = dst.at[y] if side is None else dst.at[y, side]
        for o in others:
            to = lax.rem(y + o, n)
            pltpu.make_async_remote_copy(
                src_ref=at(to),
                dst_ref=there,
                send_sem=out_send.at[index],
                recv_sem=out_recv.at[index % 3 and 1],
                device_id=(to_ctx, to),
                device_id_type=MESH,
            ).start()
        if 0 not in others:
            pltpu.make_async_copy(at(y), there, out_recv.at[index % 3 and 1]).start()

    lax.fori_loop(0, 2, make_step, 0)
    take(FAR)
    pass_on(FAR)
    take(0)
    pass_ahead_0()
    make_side(0)
    deliver(0, dq_out.at[0], gq_out, me, offsets, 0)
    make_side(1)
    take(3)
    pass_on(3)
    take(1)
    pass_ahead_1()
    deliver(3, dq_out.at[1], gq_out, me, offsets, 1)
    take(2)

    @pl.when(chip >= 2)
    def _():
        for piece in pieces:
            ahead(piece, 1).wait_recv()

            @pl.when(chip < last)
            def _():
                back(piece, 3).wait_recv()

            added(piece, 2, ahead_in.at[1], back_in.at[2])
        deliver(1, back_out.at[2], gkv_out, source, offsets + [0])

    @pl.when(chip >= last - 1)
    def _():
        for piece in pieces:
            @pl.when(chip == last - 1)
            def _():
                back(piece, 1).wait_recv()

            added(piece, 0, back_in.at[0])
        deliver(2, back_out.at[0], gkv_out, me, offsets)

    for index, ref in enumerate((gq_out, gkv_out)):
        got(ref, out_recv.at[index])

    @pl.when(chip == last)
    def _():
        got(kv_stage.at[:, :, pl.ds(0, (n - 1) * HEAD)], in_send.at[0])

    @pl.when(chip > 0)
    def _():
        give_back().wait_send()

    @pl.when(chip < last)
    def _():
        got(kv_stage, in_send.at[2])

    for index in (1, 3):
        got(qc_stage.at[:, :, pl.ds(0, (n - 1) * wide // 2)], in_send.at[index])
    for side in range(2):
        got(dq_out.at[side, pl.ds(0, (n - 1) * rows), :], out_send.at[3 * side])

    @pl.when(chip >= 2)
    def _():
        got(back_out.at[2], out_send.at[1])

    @pl.when(chip >= last - 1)
    def _():
        got(back_out.at[0, :, pl.ds(0, (n - 1) * rows), :], out_send.at[2])

    @pl.when(chip < last - 1)
    def _():
        for piece in pieces:
            ahead(piece, 0).wait_send()

    @pl.when((chip >= 1) & (chip < last))
    def _():
        for piece in pieces:
            ahead(piece, 1).wait_send()

    @pl.when(chip == last)
    def _():
        for piece in pieces:
            back(piece, 1).wait_send()

    for step in range(FAR + 1):
        @pl.when(chip >= step)
        def _():
            for piece in pieces:
                share(piece, step).wait_send()
                if step > 2:
                    back(piece, step).wait_send()

        if 0 < step < FAR:
            @pl.when((chip >= step) & (chip < last))
            def _():
                for piece in pieces:
                    forward(piece, step).wait_send()

    for step in range(FAR + 1):
        @pl.when(gives(step))
        def _():
            hand_over(step).wait_send()


def finish(gq_in, gkv_in, gq_out, gk_out, gv_out, gq_blk, gkv_blk, load_sems, store_sems):
    n, sides, rows, half = gq_in.shape
    blocks = (gkv_blk.at[0], gkv_blk.at[1], gq_blk)
    for p in range(n):
        for index in range(2):
            pltpu.make_async_copy(
                gkv_in.at[p, index],
                blocks[index].at[:, p * HEAD : (p + 1) * HEAD],
                load_sems.at[index],
            ).start()
        for side in range(sides):
            at = (p * sides + side) * half
            pltpu.make_async_copy(
                gq_in.at[p, side], gq_blk.at[:, at : at + half], load_sems.at[2]
            ).start()
    stores = [
        pltpu.make_async_copy(blocks[index], dst, store_sems.at[index])
        for index, dst in enumerate((gk_out, gv_out, gq_out))
    ]
    for index in range(3):
        pltpu.make_async_copy(blocks[index], blocks[index], load_sems.at[index]).wait()
        stores[index].start()
    for store in stores:
        store.wait()


def shards(queries, keys, values, grad_out, doc_lengths):
    n = lax.axis_size("tp")
    rows = queries.shape[0]
    block = rows * n
    wide = queries.shape[1] // n
    group = wide // HEAD
    blocks = 2 * FAR + 1
    bf16, f32 = jnp.bfloat16, jnp.float32
    vmem = pltpu.VMEM
    dma = pltpu.SemaphoreType.DMA
    any_spec = pl.BlockSpec(memory_space=pl.ANY)
    like_q = jax.ShapeDtypeStruct(queries.shape, bf16)
    like_k = jax.ShapeDtypeStruct(keys.shape, bf16)
    split_q = jax.ShapeDtypeStruct((n, 2, rows, wide // 2), bf16)
    split_kv = jax.ShapeDtypeStruct((n, 2, rows, HEAD), bf16)
    parts = pl.pallas_call(
        kernel,
        out_shape=[split_q, split_kv],
        in_specs=[any_spec] * 4 + [pl.BlockSpec(memory_space=pltpu.SMEM)],
        out_specs=[any_spec] * 2,
        scratch_shapes=[
            vmem((2, *queries.shape), bf16),
            vmem((2, *keys.shape), bf16),
            vmem((2, block, wide), bf16),
            vmem((2 * FAR + 2, 2, block, HEAD), bf16),
            vmem((blocks * group, block, block), f32),
            vmem((blocks * group, block, block), f32),
            vmem((blocks * group, 1, block), f32),
            vmem((1, block), jnp.int32),
            vmem((group, HEAD, block), f32),
            vmem((2, block, wide // 2), bf16),
            vmem((FAR + 1, 2, block, HEAD), f32),
            vmem((FAR, 2, block, HEAD), f32),
            vmem((FAR + 1, 2, block, HEAD), bf16),
            vmem((FAR + 1, 2, block, HEAD), bf16),
            vmem((FAR + 1, 2, block, HEAD), bf16),
            vmem((FAR, 2, block, HEAD), bf16),
            vmem((2, 2, block, HEAD), bf16),
            dma((4,)),
            dma((2,)),
            dma((4,)),
            dma((4,)),
            dma((FAR, 2, HALVES)),
            dma((FAR, 2, HALVES)),
            dma((FAR + 1, 2, HALVES)),
            dma((FAR + 1, 2, HALVES)),
            dma((FAR, 2, HALVES)),
            dma((FAR, 2, HALVES)),
            dma((2, 2, HALVES)),
            dma((2, 2, HALVES)),
            dma((FAR + 1,)),
            dma((FAR + 1,)),
            dma((4,)),
            dma((2,)),
        ],
        compiler_params=pltpu.CompilerParams(
            collective_id=0, has_side_effects=True, vmem_limit_bytes=60 * 2**20
        ),
    )(queries, keys, values, grad_out, doc_lengths)
    return pl.pallas_call(
        finish,
        out_shape=[like_q, like_k, like_k],
        in_specs=[any_spec] * 2,
        out_specs=[any_spec] * 3,
        scratch_shapes=[
            vmem(queries.shape, bf16),
            vmem((2, *keys.shape), bf16),
            dma((3,)),
            dma((3,)),
        ],
        compiler_params=pltpu.CompilerParams(vmem_limit_bytes=60 * 2**20),
    )(*parts)


def solution(mesh):
    placed = P(("ctx", "tp"), None)
    return jax.shard_map(
        shards,
        mesh=mesh,
        in_specs=(placed,) * 4 + (P(),),
        out_specs=(placed,) * 3,
        check_vma=False,
    )
```

```python
import functools

import jax
import jax.numpy as jnp
from jax import lax
from jax.experimental import pallas as pl
from jax.experimental.pallas import tpu as pltpu
from jax.sharding import PartitionSpec as P

HEAD = 128
FAR = 4
HALVES = 2
MESH = pl.DeviceIdType.MESH
LOG2E = 1.4426950408889634
LOW = -1e30

NT = (((1,), (1,)), ((), ()))


def dot(a, b, dims=(((1,), (0,)), ((), ()))):
    return lax.dot_general(a, b, dims, preferred_element_type=jnp.float32)


def kernel(
    q_in, k_in, v_in, c_in, lengths,
    gq_out, gkv_out,
    qc_stage, kv_stage, qc_blk, kv_win, weights, dprobs, tops, starts,
    dq_acc, dq_out, own, sib_acc, sib_out, sib_in, back_out, back_in, ahead_in,
    stage_sem, home_sem, in_send, in_recv, fwd_send, fwd_recv, pair_send, pair_recv,
    back_send, back_recv, ahead_send, ahead_recv, term_send, term_recv, out_send, out_recv,
):
    n = lax.axis_size("tp")
    ring = lax.axis_size("ctx")
    me = lax.axis_index("ctx")
    y = lax.axis_index("tp")
    core = lax.rem(me, 2)
    chip = me // 2
    last = ring // 2 - 1
    after = lax.rem(me + 2, ring)
    before = lax.rem(me + ring - 2, ring)
    source = lax.rem(me + ring - 4, ring)
    twin = me + 1 - 2 * core
    rows = q_in.shape[0]
    block = rows * n
    half = block // HALVES
    wide = qc_blk.shape[2]
    group = wide // HEAD
    factor = HEAD ** -0.5
    scale = factor * LOG2E
    mine = 1 - core
    offsets = sorted(range(1, n), key=lambda o: -min(o, n - o))

    barrier = pltpu.get_barrier_semaphore()
    for o in offsets:
        pl.semaphore_signal(
            barrier, inc=1, device_id=(me, lax.rem(y + o, n)), device_id_type=MESH
        )
        pl.semaphore_signal(
            barrier, inc=1, device_id=(before, lax.rem(y + o, n)), device_id_type=MESH
        )
    for other in (before, twin):
        pl.semaphore_signal(barrier, inc=1, device_id=(other, y), device_id_type=MESH)

    staged = (
        (k_in, kv_stage.at[0]),
        (v_in, kv_stage.at[1]),
        (q_in, qc_stage.at[0]),
        (c_in, qc_stage.at[1]),
    )
    for index, (src, dst) in enumerate(staged):
        pltpu.make_async_copy(src, dst, stage_sem.at[index]).start()

    position = me * block + lax.broadcasted_iota(jnp.int32, (1, block), 1)
    begin = jnp.zeros((1, block), jnp.int32)
    end = jnp.int32(0)
    for d in range(lengths.shape[0]):
        end = end + lengths[d]
        begin = jnp.where(position >= end, end, begin)
    starts[...] = begin
    key_row = lax.broadcasted_iota(jnp.int32, (block, block), 0)
    query_lane = lax.broadcasted_iota(jnp.int32, (block, block), 1)
    dq_acc[...] = jnp.zeros_like(dq_acc)

    for step in range(1, FAR + 1):
        @pl.when(chip < step)
        def _():
            kv_win[2 * step : 2 * step + 2] = jnp.zeros((2, *kv_win.shape[1:]), kv_win.dtype)

    @pl.when(chip == last)
    def _():
        back_in[...] = jnp.zeros_like(back_in)


    for index, (src, dst) in enumerate(staged):
        pltpu.make_async_copy(src, dst, stage_sem.at[index]).wait()
    pl.semaphore_wait(barrier, 2 * n)

    here = pl.ds(pl.multiple_of(y * rows, rows), rows)

    def spread(index, src, width, dst, to_ctx, others):
        def of(p):
            columns = pl.ds(pl.multiple_of(p * width, width), width)
            return src.at[:, :, columns] if len(src.shape) == 3 else src.at[:, columns]

        for o in others:
            to = lax.rem(y + o, n)
            pltpu.make_async_remote_copy(
                src_ref=of(to),
                dst_ref=dst,
                send_sem=in_send.at[index],
                recv_sem=in_recv.at[index],
                device_id=(to_ctx, to),
                device_id_type=MESH,
            ).start()
        if 0 not in others:
            pltpu.make_async_copy(of(y), dst, in_recv.at[index]).start()

    @pl.when(chip < last)
    def _():
        for index in range(2):
            dst = kv_win.at[mine + 2, index, here, :]
            spread(2 + 2 * index, kv_stage.at[index], HEAD, dst, after, offsets + [0])

    @pl.when(chip == last)
    def _():
        spread(0, kv_stage, HEAD, kv_win.at[mine, :, here, :], me, offsets)

    def side_sem(h):
        return 1 if h < group // 2 else 3

    for h in range(group):
        for o in offsets + [0]:
            to = lax.rem(y + o, n)
            src = qc_stage.at[:, :, pl.ds(pl.multiple_of(to * wide + h * HEAD, HEAD), HEAD)]
            dst = qc_blk.at[:, here, h * HEAD : (h + 1) * HEAD]
            if o:
                pltpu.make_async_remote_copy(
                    src_ref=src,
                    dst_ref=dst,
                    send_sem=in_send.at[side_sem(h)],
                    recv_sem=in_recv.at[side_sem(h)],
                    device_id=(me, to),
                    device_id_type=MESH,
                ).start()
            else:
                pltpu.make_async_copy(src, dst, in_recv.at[side_sem(h)]).start()

    def got(ref, sem):
        pltpu.make_async_copy(ref, ref, sem).wait()

    pieces = [(index, part) for index in range(2) for part in range(HALVES)]

    def forward(piece, step):
        index, part = piece
        at = 2 * step + mine
        span = pl.ds(part * half, half)
        return pltpu.make_async_remote_copy(
            src_ref=kv_win.at[at, index, span],
            dst_ref=kv_win.at[at + 2, index, span],
            send_sem=fwd_send.at[step, index, part],
            recv_sem=fwd_recv.at[step, index, part],
            device_id=(after, y),
            device_id_type=MESH,
        )

    def share(piece, step):
        index, part = piece
        at = 2 * step + mine
        span = pl.ds(part * half, half)
        return pltpu.make_async_remote_copy(
            src_ref=kv_win.at[at, index, span],
            dst_ref=kv_win.at[at, index, span],
            send_sem=pair_send.at[step, index, part],
            recv_sem=pair_recv.at[step, index, part],
            device_id=(twin, y),
            device_id_type=MESH,
        )

    def relay(step):
        @pl.when(chip >= step)
        def _():
            for piece in pieces:
                if step == 1 and piece[1] == 0:
                    got(kv_win.at[mine + 2, piece[0]], in_recv.at[2 + 2 * piece[0]])
                if step > 1:
                    forward(piece, step - 1).wait_recv()
                if step < FAR:
                    @pl.when(chip < last)
                    def _():
                        forward(piece, step).start()

                share(piece, step).start()

    def give_back():
        return pltpu.make_async_remote_copy(
            src_ref=kv_win.at[mine + 2],
            dst_ref=kv_win.at[mine],
            send_sem=home_sem.at[0],
            recv_sem=home_sem.at[1],
            device_id=(before, y),
            device_id_type=MESH,
        )

    def shared(step):
        @pl.when(chip >= step)
        def _():
            for piece in pieces:
                share(piece, step).wait_recv()

    def of_head(index, h):
        return qc_blk[index, :, h * HEAD : (h + 1) * HEAD]

    def scan_blocks(fars, heads, carry, diagonal=False):
        allowed = []
        for far in fars:
            inside = key_row >= starts[...] - (me - far) * block
            allowed.append(inside & (key_row <= query_lane) if diagonal else inside)
        new = []
        for j, h in enumerate(heads):
            scores = []
            for far, inside in zip(fars, allowed):
                s = dot(kv_win[far + mine, 0], of_head(0, h), NT)
                scores.append(jnp.where(inside, s, LOW))
            tops_here = [jnp.max(s, axis=0, keepdims=True) for s in scores]
            if not diagonal:
                tops_here.append(carry[j][0])
            top = functools.reduce(jnp.maximum, tops_here)
            total = jnp.zeros((1, block), jnp.float32)
            weighted = jnp.zeros((1, block), jnp.float32)
            if not diagonal:
                old, total, weighted = carry[j]
                shrink = jnp.exp2((old - top) * scale)
                total = total * shrink
                weighted = weighted * shrink
            for far, s in zip(fars, scores):
                dp = dot(kv_win[far + mine, 1], of_head(1, h), NT)
                e = jnp.exp2(s * scale - top * scale)
                total = total + jnp.sum(e, axis=0, keepdims=True)
                weighted = weighted + jnp.sum(e * dp, axis=0, keepdims=True)
                weights[far * group + h] = e
                dprobs[far * group + h] = dp
                tops[far * group + h] = top
            new.append((top, total, weighted))
        return tuple(new)

    def scan_side(heads):
        carry = scan_blocks((0,), heads, None, True)
        return lax.fori_loop(
            0, FAR - 1, lambda i, c: scan_blocks((2 * i + 1, 2 * i + 2), heads, c), carry
        )

    relay(1)

    @pl.when(chip > 0)
    def _():
        give_back().start()

    relay(2)

    @pl.when(chip < last)
    def _():
        give_back().wait_recv()

    @pl.when(chip == last)
    def _():
        got(kv_win.at[mine], in_recv.at[0])

    for piece in pieces:
        share(piece, 0).start()
    relay(3)
    for step in range(FAR):
        shared(step)
    stats = ()
    sides = [tuple(range(i * group // 2, (i + 1) * group // 2)) for i in range(2)]
    for heads in sides:
        sem = in_recv.at[side_sem(heads[0])]
        got(qc_blk.at[:, :, heads[0] * HEAD : (heads[-1] + 1) * HEAD], sem)
        stats += scan_side(heads)
    relay(FAR)
    stats = scan_blocks((2 * FAR,), range(group), stats)
    shared(FAR)
    stats = scan_blocks((2 * FAR - 1,), range(group), stats)

    def terms(far, heads):
        at = far + mine
        k_t = kv_win[at, 0].T
        dk = jnp.zeros((block, HEAD), jnp.float32)
        dv = jnp.zeros((block, HEAD), jnp.float32)
        for h in heads:
            top, total, weighted = stats[h]
            inv = 1.0 / total
            shrink = jnp.exp2((tops[far * group + h] - top) * scale) * inv
            p = weights[far * group + h] * shrink
            ds = (p * (dprobs[far * group + h] - weighted * inv)).astype(jnp.bfloat16)
            dv = dv + dot(p.astype(jnp.bfloat16), of_head(1, h))
            dk = dk + dot(ds, of_head(0, h))
            dq_acc[h] += dot(k_t, ds)
        return dk, dv

    def hand_over(step):
        return pltpu.make_async_remote_copy(
            src_ref=sib_out.at[step],
            dst_ref=sib_in.at[step],
            send_sem=term_send.at[step],
            recv_sem=term_recv.at[step],
            device_id=(twin, y),
            device_id_type=MESH,
        )

    def back(piece, step):
        index, part = piece
        span = pl.ds(part * half, half)
        return pltpu.make_async_remote_copy(
            src_ref=back_out.at[step, index, span],
            dst_ref=back_in.at[step - 1, index, span],
            send_sem=back_send.at[step - 1, index, part],
            recv_sem=back_recv.at[step - 1, index, part],
            device_id=(before, y),
            device_id_type=MESH,
        )

    def gives(step):
        return (step >= 1 - core) & (step <= FAR - core)

    def takes(step):
        return (step >= core) & (step <= FAR - 1 + core)

    def make_terms(step):
        @pl.when(gives(step))
        def _():
            for index, term in enumerate(terms(2 * step - 1 + 2 * core, range(group))):
                sib_out[step, index] = term.astype(jnp.bfloat16)
            hand_over(step).start()

        for index, term in enumerate(terms(2 * step, range(group))):
            own[step, index] = term

    def take(step):
        @pl.when(takes(step))
        def _():
            hand_over(step).wait_recv()
            own[step] += sib_in[step].astype(jnp.float32)

    def ahead(piece, step):
        index, part = piece
        span = pl.ds(part * half, half)
        return pltpu.make_async_remote_copy(
            src_ref=back_out.at[step, index, span],
            dst_ref=ahead_in.at[step, index, span],
            send_sem=ahead_send.at[step, index, part],
            recv_sem=ahead_recv.at[step, index, part],
            device_id=(after, y),
            device_id_type=MESH,
        )

    def added(piece, step, *more):
        index, part = piece
        span = pl.ds(part * half, half)
        sums = own[step, index, span]
        for ref in more:
            sums = sums + ref[index, span].astype(jnp.float32)
        if step in (0, 2) and index == 0:
            sums = sums * factor
        back_out[step, index, span] = sums.astype(jnp.bfloat16)

    def pass_on(step):
        @pl.when(chip >= step)
        def _():
            for piece in pieces:
                if step < FAR:
                    @pl.when(chip < last)
                    def _():
                        back(piece, step + 1).wait_recv()

                    added(piece, step, back_in.at[step])
                else:
                    added(piece, step)
                back(piece, step).start()

    def pass_ahead_0():
        @pl.when(chip < last - 1)
        def _():
            for index, part in pieces:
                span = pl.ds(part * half, half)
                back_out[0, index, span] = own[0, index, span].astype(jnp.bfloat16)
                ahead((index, part), 0).start()

    def pass_ahead_1():
        @pl.when((chip >= 1) & (chip < last))
        def _():
            for piece in pieces:
                ahead(piece, 0).wait_recv()
                added(piece, 1, ahead_in.at[0])
                ahead(piece, 1).start()

        @pl.when(chip == last)
        def _():
            for piece in pieces:
                added(piece, 1)
                back(piece, 1).start()

    def make_step(i, carry):
        make_terms(FAR * (1 - i))
        return carry

    def make_side(side):
        heads = sides[side]

        def step_of(i, carry):
            step = jnp.where(i == 0, 3, i)
            other = terms(2 * step - 1 + 2 * core, heads)
            same = terms(2 * step, heads)
            for index in range(2):
                if side == 0:
                    sib_acc[step, index] = other[index]
                    own[step, index] = same[index]
                else:
                    sib_out[step, index] = (sib_acc[step, index] + other[index]).astype(jnp.bfloat16)
                    own[step, index] += same[index]
            if side == 1:
                hand_over(step).start()
            return carry

        lax.fori_loop(0, 3, step_of, 0)
        for h in heads:
            dq_out[side, :, (h - heads[0]) * HEAD : (h - heads[0] + 1) * HEAD] = (
                (dq_acc[h] * factor).T.astype(jnp.bfloat16)
            )

    def deliver(index, src, dst, to_ctx, others, side=None):
        def at(p):
            rows_of = pl.ds(pl.multiple_of(p * rows, rows), rows)
            return src.at[:, rows_of, :] if len(src.shape) == 3 else src.at[rows_of, :]

        there = dst.at[y] if side is None else dst.at[y, side]
        for o in others:
            to = lax.rem(y + o, n)
            pltpu.make_async_remote_copy(
                src_ref=at(to),
                dst_ref=there,
                send_sem=out_send.at[index],
                recv_sem=out_recv.at[index % 3 and 1],
                device_id=(to_ctx, to),
                device_id_type=MESH,
            ).start()
        if 0 not in others:
            pltpu.make_async_copy(at(y), there, out_recv.at[index % 3 and 1]).start()

    lax.fori_loop(0, 2, make_step, 0)
    take(FAR)
    pass_on(FAR)
    take(0)
    pass_ahead_0()
    make_side(0)
    deliver(0, dq_out.at[0], gq_out, me, offsets, 0)
    make_side(1)
    take(3)
    pass_on(3)
    take(1)
    pass_ahead_1()
    deliver(3, dq_out.at[1], gq_out, me, offsets, 1)
    take(2)

    @pl.when(chip >= 2)
    def _():
        for piece in pieces:
            ahead(piece, 1).wait_recv()

            @pl.when(chip < last)
            def _():
                back(piece, 3).wait_recv()

            added(piece, 2, ahead_in.at[1], back_in.at[2])
            index, part = piece
            if part == HALVES - 1:
                deliver(1, back_out.at[2, index], gkv_out, source, offsets + [0], index)

    @pl.when(chip >= last - 1)
    def _():
        for piece in pieces:
            @pl.when(chip == last - 1)
            def _():
                back(piece, 1).wait_recv()

            added(piece, 0, back_in.at[0])
        deliver(2, back_out.at[0], gkv_out, me, offsets)

    for index, ref in enumerate((gq_out, gkv_out)):
        got(ref, out_recv.at[index])

    @pl.when(chip == last)
    def _():
        got(kv_stage.at[:, :, pl.ds(0, (n - 1) * HEAD)], in_send.at[0])

    @pl.when(chip > 0)
    def _():
        give_back().wait_send()

    @pl.when(chip < last)
    def _():
        for index in range(2):
            got(kv_stage.at[index], in_send.at[2 + 2 * index])

    for index in (1, 3):
        got(qc_stage.at[:, :, pl.ds(0, (n - 1) * wide // 2)], in_send.at[index])
    for side in range(2):
        got(dq_out.at[side, pl.ds(0, (n - 1) * rows), :], out_send.at[3 * side])

    @pl.when(chip >= 2)
    def _():
        got(back_out.at[2], out_send.at[1])

    @pl.when(chip >= last - 1)
    def _():
        got(back_out.at[0, :, pl.ds(0, (n - 1) * rows), :], out_send.at[2])

    @pl.when(chip < last - 1)
    def _():
        for piece in pieces:
            ahead(piece, 0).wait_send()

    @pl.when((chip >= 1) & (chip < last))
    def _():
        for piece in pieces:
            ahead(piece, 1).wait_send()

    @pl.when(chip == last)
    def _():
        for piece in pieces:
            back(piece, 1).wait_send()

    for step in range(FAR + 1):
        @pl.when(chip >= step)
        def _():
            for piece in pieces:
                share(piece, step).wait_send()
                if step > 2:
                    back(piece, step).wait_send()

        if 0 < step < FAR:
            @pl.when((chip >= step) & (chip < last))
            def _():
                for piece in pieces:
                    forward(piece, step).wait_send()

    for step in range(FAR + 1):
        @pl.when(gives(step))
        def _():
            hand_over(step).wait_send()


def finish(gq_in, gkv_in, gq_out, gk_out, gv_out, gq_blk, gkv_blk, load_sems, store_sems):
    n, sides, rows, half = gq_in.shape
    blocks = (gkv_blk.at[0], gkv_blk.at[1], gq_blk)
    for p in range(n):
        for index in range(2):
            pltpu.make_async_copy(
                gkv_in.at[p, index],
                blocks[index].at[:, p * HEAD : (p + 1) * HEAD],
                load_sems.at[index],
            ).start()
        for side in range(sides):
            at = (p * sides + side) * half
            pltpu.make_async_copy(
                gq_in.at[p, side], gq_blk.at[:, at : at + half], load_sems.at[2]
            ).start()
    stores = [
        pltpu.make_async_copy(blocks[index], dst, store_sems.at[index])
        for index, dst in enumerate((gk_out, gv_out, gq_out))
    ]
    for index in range(3):
        pltpu.make_async_copy(blocks[index], blocks[index], load_sems.at[index]).wait()
        stores[index].start()
    for store in stores:
        store.wait()


def shards(queries, keys, values, grad_out, doc_lengths):
    n = lax.axis_size("tp")
    rows = queries.shape[0]
    block = rows * n
    wide = queries.shape[1] // n
    group = wide // HEAD
    blocks = 2 * FAR + 1
    bf16, f32 = jnp.bfloat16, jnp.float32
    vmem = pltpu.VMEM
    dma = pltpu.SemaphoreType.DMA
    any_spec = pl.BlockSpec(memory_space=pl.ANY)
    like_q = jax.ShapeDtypeStruct(queries.shape, bf16)
    like_k = jax.ShapeDtypeStruct(keys.shape, bf16)
    split_q = jax.ShapeDtypeStruct((n, 2, rows, wide // 2), bf16)
    split_kv = jax.ShapeDtypeStruct((n, 2, rows, HEAD), bf16)
    parts = pl.pallas_call(
        kernel,
        out_shape=[split_q, split_kv],
        in_specs=[any_spec] * 4 + [pl.BlockSpec(memory_space=pltpu.SMEM)],
        out_specs=[any_spec] * 2,
        scratch_shapes=[
            vmem((2, *queries.shape), bf16),
            vmem((2, *keys.shape), bf16),
            vmem((2, block, wide), bf16),
            vmem((2 * FAR + 2, 2, block, HEAD), bf16),
            vmem((blocks * group, block, block), f32),
            vmem((blocks * group, block, block), f32),
            vmem((blocks * group, 1, block), f32),
            vmem((1, block), jnp.int32),
            vmem((group, HEAD, block), f32),
            vmem((2, block, wide // 2), bf16),
            vmem((FAR + 1, 2, block, HEAD), f32),
            vmem((FAR, 2, block, HEAD), f32),
            vmem((FAR + 1, 2, block, HEAD), bf16),
            vmem((FAR + 1, 2, block, HEAD), bf16),
            vmem((FAR + 1, 2, block, HEAD), bf16),
            vmem((FAR, 2, block, HEAD), bf16),
            vmem((2, 2, block, HEAD), bf16),
            dma((4,)),
            dma((2,)),
            dma((5,)),
            dma((5,)),
            dma((FAR, 2, HALVES)),
            dma((FAR, 2, HALVES)),
            dma((FAR + 1, 2, HALVES)),
            dma((FAR + 1, 2, HALVES)),
            dma((FAR, 2, HALVES)),
            dma((FAR, 2, HALVES)),
            dma((2, 2, HALVES)),
            dma((2, 2, HALVES)),
            dma((FAR + 1,)),
            dma((FAR + 1,)),
            dma((4,)),
            dma((2,)),
        ],
        compiler_params=pltpu.CompilerParams(
            collective_id=0, has_side_effects=True, vmem_limit_bytes=60 * 2**20
        ),
    )(queries, keys, values, grad_out, doc_lengths)
    return pl.pallas_call(
        finish,
        out_shape=[like_q, like_k, like_k],
        in_specs=[any_spec] * 2,
        out_specs=[any_spec] * 3,
        scratch_shapes=[
            vmem(queries.shape, bf16),
            vmem((2, *keys.shape), bf16),
            dma((3,)),
            dma((3,)),
        ],
        compiler_params=pltpu.CompilerParams(vmem_limit_bytes=60 * 2**20),
    )(*parts)


def solution(mesh):
    placed = P(("ctx", "tp"), None)
    return jax.shard_map(
        shards,
        mesh=mesh,
        in_specs=(placed,) * 4 + (P(),),
        out_specs=(placed,) * 3,
        check_vma=False,
    )
```

```python
import functools

import jax
import jax.numpy as jnp
from jax import lax
from jax.experimental import pallas as pl
from jax.experimental.pallas import tpu as pltpu
from jax.sharding import PartitionSpec as P

HEAD = 128
FAR = 4
HALVES = 2
MESH = pl.DeviceIdType.MESH
LOG2E = 1.4426950408889634
LOW = -1e30

NT = (((1,), (1,)), ((), ()))


def dot(a, b, dims=(((1,), (0,)), ((), ()))):
    return lax.dot_general(a, b, dims, preferred_element_type=jnp.float32)


def kernel(
    q_in, k_in, v_in, c_in, lengths,
    gq_out, gkv_out,
    qc_stage, kv_stage, qc_blk, kv_win, weights, dprobs, tops, starts,
    dq_acc, dq_out, own, sib_acc, sib_out, sib_in, back_out, back_in, ahead_in,
    stage_sem, home_sem, in_send, in_recv, fwd_send, fwd_recv, pair_send, pair_recv,
    back_send, back_recv, ahead_send, ahead_recv, term_send, term_recv, out_send, out_recv,
):
    n = lax.axis_size("tp")
    ring = lax.axis_size("ctx")
    me = lax.axis_index("ctx")
    y = lax.axis_index("tp")
    core = lax.rem(me, 2)
    chip = me // 2
    last = ring // 2 - 1
    after = lax.rem(me + 2, ring)
    before = lax.rem(me + ring - 2, ring)
    source = lax.rem(me + ring - 4, ring)
    twin = me + 1 - 2 * core
    rows = q_in.shape[0]
    block = rows * n
    half = block // HALVES
    wide = qc_blk.shape[2]
    group = wide // HEAD
    factor = HEAD ** -0.5
    scale = factor * LOG2E
    mine = 1 - core
    offsets = sorted(range(1, n), key=lambda o: -min(o, n - o))

    barrier = pltpu.get_barrier_semaphore()
    for o in offsets:
        pl.semaphore_signal(
            barrier, inc=1, device_id=(me, lax.rem(y + o, n)), device_id_type=MESH
        )
        pl.semaphore_signal(
            barrier, inc=1, device_id=(before, lax.rem(y + o, n)), device_id_type=MESH
        )
    for other in (before, twin):
        pl.semaphore_signal(barrier, inc=1, device_id=(other, y), device_id_type=MESH)

    staged = (
        (k_in, kv_stage.at[0]),
        (v_in, kv_stage.at[1]),
        (q_in, qc_stage.at[0]),
        (c_in, qc_stage.at[1]),
    )
    for index, (src, dst) in enumerate(staged):
        pltpu.make_async_copy(src, dst, stage_sem.at[index]).start()

    position = me * block + lax.broadcasted_iota(jnp.int32, (1, block), 1)
    begin = jnp.zeros((1, block), jnp.int32)
    end = jnp.int32(0)
    for d in range(lengths.shape[0]):
        end = end + lengths[d]
        begin = jnp.where(position >= end, end, begin)
    starts[...] = begin
    key_row = lax.broadcasted_iota(jnp.int32, (block, block), 0)
    query_lane = lax.broadcasted_iota(jnp.int32, (block, block), 1)
    dq_acc[...] = jnp.zeros_like(dq_acc)

    for step in range(1, FAR + 1):
        @pl.when(chip < step)
        def _():
            kv_win[2 * step : 2 * step + 2] = jnp.zeros((2, *kv_win.shape[1:]), kv_win.dtype)

    @pl.when(chip == last)
    def _():
        back_in[...] = jnp.zeros_like(back_in)


    for index, (src, dst) in enumerate(staged):
        pltpu.make_async_copy(src, dst, stage_sem.at[index]).wait()
    pl.semaphore_wait(barrier, 2 * n)

    here = pl.ds(pl.multiple_of(y * rows, rows), rows)

    def spread(index, src, width, dst, to_ctx, others):
        def of(p):
            columns = pl.ds(pl.multiple_of(p * width, width), width)
            return src.at[:, :, columns] if len(src.shape) == 3 else src.at[:, columns]

        for o in others:
            to = lax.rem(y + o, n)
            pltpu.make_async_remote_copy(
                src_ref=of(to),
                dst_ref=dst,
                send_sem=in_send.at[index],
                recv_sem=in_recv.at[index],
                device_id=(to_ctx, to),
                device_id_type=MESH,
            ).start()
        if 0 not in others:
            pltpu.make_async_copy(of(y), dst, in_recv.at[index]).start()

    @pl.when(chip < last)
    def _():
        for index in range(2):
            dst = kv_win.at[mine + 2, index, here, :]
            spread(2 + 2 * index, kv_stage.at[index], HEAD, dst, after, offsets + [0])

    @pl.when(chip == last)
    def _():
        spread(0, kv_stage, HEAD, kv_win.at[mine, :, here, :], me, offsets)

    def side_sem(h):
        return 1 if h < group // 2 else 3

    pair = wide // 2
    for side in range(2):
        for o in offsets + [0]:
            to = lax.rem(y + o, n)
            columns = pl.ds(pl.multiple_of(to * wide + side * pair, HEAD), pair)
            for index in range(2):
                src = qc_stage.at[index, :, columns]
                dst = qc_blk.at[index, here, side * pair : (side + 1) * pair]
                if o:
                    pltpu.make_async_remote_copy(
                        src_ref=src,
                        dst_ref=dst,
                        send_sem=in_send.at[1 + 2 * side],
                        recv_sem=in_recv.at[1 + 2 * side],
                        device_id=(me, to),
                        device_id_type=MESH,
                    ).start()
                else:
                    pltpu.make_async_copy(src, dst, in_recv.at[1 + 2 * side]).start()

    def got(ref, sem):
        pltpu.make_async_copy(ref, ref, sem).wait()

    pieces = [(index, part) for index in range(2) for part in range(HALVES)]

    def forward(piece, step):
        index, part = piece
        at = 2 * step + mine
        span = pl.ds(part * half, half)
        return pltpu.make_async_remote_copy(
            src_ref=kv_win.at[at, index, span],
            dst_ref=kv_win.at[at + 2, index, span],
            send_sem=fwd_send.at[step, index, part],
            recv_sem=fwd_recv.at[step, index, part],
            device_id=(after, y),
            device_id_type=MESH,
        )

    def share(piece, step):
        index, part = piece
        at = 2 * step + mine
        span = pl.ds(part * half, half)
        return pltpu.make_async_remote_copy(
            src_ref=kv_win.at[at, index, span],
            dst_ref=kv_win.at[at, index, span],
            send_sem=pair_send.at[step, index, part],
            recv_sem=pair_recv.at[step, index, part],
            device_id=(twin, y),
            device_id_type=MESH,
        )

    def relay(step):
        @pl.when(chip >= step)
        def _():
            for piece in pieces:
                if step == 1 and piece[1] == 0:
                    got(kv_win.at[mine + 2, piece[0]], in_recv.at[2 + 2 * piece[0]])
                if step > 1:
                    forward(piece, step - 1).wait_recv()
                if step < FAR:
                    @pl.when(chip < last)
                    def _():
                        forward(piece, step).start()

                share(piece, step).start()

    def give_back():
        return pltpu.make_async_remote_copy(
            src_ref=kv_win.at[mine + 2],
            dst_ref=kv_win.at[mine],
            send_sem=home_sem.at[0],
            recv_sem=home_sem.at[1],
            device_id=(before, y),
            device_id_type=MESH,
        )

    def shared(step):
        @pl.when(chip >= step)
        def _():
            for piece in pieces:
                share(piece, step).wait_recv()

    def of_head(index, h):
        return qc_blk[index, :, h * HEAD : (h + 1) * HEAD]

    def scan_blocks(fars, heads, carry, diagonal=False):
        allowed = []
        for far in fars:
            inside = key_row >= starts[...] - (me - far) * block
            allowed.append(inside & (key_row <= query_lane) if diagonal else inside)
        new = []
        for j, h in enumerate(heads):
            scores = []
            for far, inside in zip(fars, allowed):
                s = dot(kv_win[far + mine, 0], of_head(0, h), NT)
                scores.append(jnp.where(inside, s, LOW))
            tops_here = [jnp.max(s, axis=0, keepdims=True) for s in scores]
            if not diagonal:
                tops_here.append(carry[j][0])
            top = functools.reduce(jnp.maximum, tops_here)
            total = jnp.zeros((1, block), jnp.float32)
            weighted = jnp.zeros((1, block), jnp.float32)
            if not diagonal:
                old, total, weighted = carry[j]
                shrink = jnp.exp2((old - top) * scale)
                total = total * shrink
                weighted = weighted * shrink
            for far, s in zip(fars, scores):
                dp = dot(kv_win[far + mine, 1], of_head(1, h), NT)
                e = jnp.exp2(s * scale - top * scale)
                total = total + jnp.sum(e, axis=0, keepdims=True)
                weighted = weighted + jnp.sum(e * dp, axis=0, keepdims=True)
                weights[far * group + h] = e
                dprobs[far * group + h] = dp
                tops[far * group + h] = top
            new.append((top, total, weighted))
        return tuple(new)

    def scan_side(heads):
        carry = scan_blocks((0,), heads, None, True)
        return lax.fori_loop(
            0, FAR - 1, lambda i, c: scan_blocks((2 * i + 1, 2 * i + 2), heads, c), carry
        )

    relay(1)

    @pl.when(chip > 0)
    def _():
        give_back().start()

    relay(2)

    @pl.when(chip < last)
    def _():
        give_back().wait_recv()

    @pl.when(chip == last)
    def _():
        got(kv_win.at[mine], in_recv.at[0])

    for piece in pieces:
        share(piece, 0).start()
    relay(3)
    for step in range(FAR):
        shared(step)
    stats = ()
    sides = [tuple(range(i * group // 2, (i + 1) * group // 2)) for i in range(2)]
    for heads in sides:
        sem = in_recv.at[side_sem(heads[0])]
        got(qc_blk.at[:, :, heads[0] * HEAD : (heads[-1] + 1) * HEAD], sem)
        stats += scan_side(heads)
    relay(FAR)
    stats = scan_blocks((2 * FAR,), range(group), stats)
    shared(FAR)
    stats = scan_blocks((2 * FAR - 1,), range(group), stats)

    def terms(far, heads):
        at = far + mine
        k_t = kv_win[at, 0].T
        dk = jnp.zeros((block, HEAD), jnp.float32)
        dv = jnp.zeros((block, HEAD), jnp.float32)
        for h in heads:
            top, total, weighted = stats[h]
            inv = 1.0 / total
            shrink = jnp.exp2((tops[far * group + h] - top) * scale) * inv
            p = weights[far * group + h] * shrink
            ds = (p * (dprobs[far * group + h] - weighted * inv)).astype(jnp.bfloat16)
            dv = dv + dot(p.astype(jnp.bfloat16), of_head(1, h))
            dk = dk + dot(ds, of_head(0, h))
            dq_acc[h] += dot(k_t, ds)
        return dk, dv

    def hand_over(step):
        return pltpu.make_async_remote_copy(
            src_ref=sib_out.at[step],
            dst_ref=sib_in.at[step],
            send_sem=term_send.at[step],
            recv_sem=term_recv.at[step],
            device_id=(twin, y),
            device_id_type=MESH,
        )

    def back(piece, step):
        index, part = piece
        span = pl.ds(part * half, half)
        return pltpu.make_async_remote_copy(
            src_ref=back_out.at[step, index, span],
            dst_ref=back_in.at[step - 1, index, span],
            send_sem=back_send.at[step - 1, index, part],
            recv_sem=back_recv.at[step - 1, index, part],
            device_id=(before, y),
            device_id_type=MESH,
        )

    def gives(step):
        return (step >= 1 - core) & (step <= FAR - core)

    def takes(step):
        return (step >= core) & (step <= FAR - 1 + core)

    def make_terms(step):
        @pl.when(gives(step))
        def _():
            for index, term in enumerate(terms(2 * step - 1 + 2 * core, range(group))):
                sib_out[step, index] = term.astype(jnp.bfloat16)
            hand_over(step).start()

        for index, term in enumerate(terms(2 * step, range(group))):
            own[step, index] = term

    def take(step):
        @pl.when(takes(step))
        def _():
            hand_over(step).wait_recv()
            own[step] += sib_in[step].astype(jnp.float32)

    def ahead(piece, step):
        index, part = piece
        span = pl.ds(part * half, half)
        return pltpu.make_async_remote_copy(
            src_ref=back_out.at[step, index, span],
            dst_ref=ahead_in.at[step, index, span],
            send_sem=ahead_send.at[step, index, part],
            recv_sem=ahead_recv.at[step, index, part],
            device_id=(after, y),
            device_id_type=MESH,
        )

    def added(piece, step, *more):
        index, part = piece
        span = pl.ds(part * half, half)
        sums = own[step, index, span]
        for ref in more:
            sums = sums + ref[index, span].astype(jnp.float32)
        if step in (0, 2) and index == 0:
            sums = sums * factor
        back_out[step, index, span] = sums.astype(jnp.bfloat16)

    def pass_on(step):
        @pl.when(chip >= step)
        def _():
            for piece in pieces:
                if step < FAR:
                    @pl.when(chip < last)
                    def _():
                        back(piece, step + 1).wait_recv()

                    added(piece, step, back_in.at[step])
                else:
                    added(piece, step)
                back(piece, step).start()

    def pass_ahead_0():
        @pl.when(chip < last - 1)
        def _():
            for index, part in pieces:
                span = pl.ds(part * half, half)
                back_out[0, index, span] = own[0, index, span].astype(jnp.bfloat16)
                ahead((index, part), 0).start()

    def pass_ahead_1():
        @pl.when((chip >= 1) & (chip < last))
        def _():
            for piece in pieces:
                ahead(piece, 0).wait_recv()
                added(piece, 1, ahead_in.at[0])
                ahead(piece, 1).start()

        @pl.when(chip == last)
        def _():
            for piece in pieces:
                added(piece, 1)
                back(piece, 1).start()

    def make_step(i, carry):
        make_terms(FAR * (1 - i))
        return carry

    def make_side(side):
        heads = sides[side]

        def step_of(i, carry):
            step = jnp.where(i == 0, 3, i)
            other = terms(2 * step - 1 + 2 * core, heads)
            same = terms(2 * step, heads)
            for index in range(2):
                if side == 0:
                    sib_acc[step, index] = other[index]
                    own[step, index] = same[index]
                else:
                    sib_out[step, index] = (sib_acc[step, index] + other[index]).astype(jnp.bfloat16)
                    own[step, index] += same[index]
            if side == 1:
                hand_over(step).start()
            return carry

        lax.fori_loop(0, 3, step_of, 0)
        for h in heads:
            dq_out[side, :, (h - heads[0]) * HEAD : (h - heads[0] + 1) * HEAD] = (
                (dq_acc[h] * factor).T.astype(jnp.bfloat16)
            )

    def deliver(index, src, dst, to_ctx, others, side=None):
        def at(p):
            rows_of = pl.ds(pl.multiple_of(p * rows, rows), rows)
            return src.at[:, rows_of, :] if len(src.shape) == 3 else src.at[rows_of, :]

        there = dst.at[y] if side is None else dst.at[y, side]
        for o in others:
            to = lax.rem(y + o, n)
            pltpu.make_async_remote_copy(
                src_ref=at(to),
                dst_ref=there,
                send_sem=out_send.at[index],
                recv_sem=out_recv.at[index % 3 and 1],
                device_id=(to_ctx, to),
                device_id_type=MESH,
            ).start()
        if 0 not in others:
            pltpu.make_async_copy(at(y), there, out_recv.at[index % 3 and 1]).start()

    lax.fori_loop(0, 2, make_step, 0)
    take(FAR)
    pass_on(FAR)
    take(0)
    pass_ahead_0()
    make_side(0)
    deliver(0, dq_out.at[0], gq_out, me, offsets, 0)
    make_side(1)
    take(3)
    pass_on(3)
    take(1)
    pass_ahead_1()
    deliver(3, dq_out.at[1], gq_out, me, offsets, 1)
    take(2)

    @pl.when(chip >= 2)
    def _():
        for piece in pieces:
            ahead(piece, 1).wait_recv()

            @pl.when(chip < last)
            def _():
                back(piece, 3).wait_recv()

            added(piece, 2, ahead_in.at[1], back_in.at[2])
            index, part = piece
            if part == HALVES - 1:
                deliver(1, back_out.at[2, index], gkv_out, source, offsets + [0], index)

    @pl.when(chip >= last - 1)
    def _():
        for piece in pieces:
            @pl.when(chip == last - 1)
            def _():
                back(piece, 1).wait_recv()

            added(piece, 0, back_in.at[0])
        deliver(2, back_out.at[0], gkv_out, me, offsets)

    for index, ref in enumerate((gq_out, gkv_out)):
        got(ref, out_recv.at[index])

    @pl.when(chip == last)
    def _():
        got(kv_stage.at[:, :, pl.ds(0, (n - 1) * HEAD)], in_send.at[0])

    @pl.when(chip > 0)
    def _():
        give_back().wait_send()

    @pl.when(chip < last)
    def _():
        for index in range(2):
            got(kv_stage.at[index], in_send.at[2 + 2 * index])

    for index in (1, 3):
        got(qc_stage.at[:, :, pl.ds(0, (n - 1) * wide // 2)], in_send.at[index])
    for side in range(2):
        got(dq_out.at[side, pl.ds(0, (n - 1) * rows), :], out_send.at[3 * side])

    @pl.when(chip >= 2)
    def _():
        got(back_out.at[2], out_send.at[1])

    @pl.when(chip >= last - 1)
    def _():
        got(back_out.at[0, :, pl.ds(0, (n - 1) * rows), :], out_send.at[2])

    @pl.when(chip < last - 1)
    def _():
        for piece in pieces:
            ahead(piece, 0).wait_send()

    @pl.when((chip >= 1) & (chip < last))
    def _():
        for piece in pieces:
            ahead(piece, 1).wait_send()

    @pl.when(chip == last)
    def _():
        for piece in pieces:
            back(piece, 1).wait_send()

    for step in range(FAR + 1):
        @pl.when(chip >= step)
        def _():
            for piece in pieces:
                share(piece, step).wait_send()
                if step > 2:
                    back(piece, step).wait_send()

        if 0 < step < FAR:
            @pl.when((chip >= step) & (chip < last))
            def _():
                for piece in pieces:
                    forward(piece, step).wait_send()

    for step in range(FAR + 1):
        @pl.when(gives(step))
        def _():
            hand_over(step).wait_send()


def finish(gq_in, gkv_in, gq_out, gk_out, gv_out, gq_blk, gkv_blk, load_sems, store_sems):
    n, sides, rows, half = gq_in.shape
    blocks = (gkv_blk.at[0], gkv_blk.at[1], gq_blk)
    for p in range(n):
        for index in range(2):
            pltpu.make_async_copy(
                gkv_in.at[p, index],
                blocks[index].at[:, p * HEAD : (p + 1) * HEAD],
                load_sems.at[index],
            ).start()
        for side in range(sides):
            at = (p * sides + side) * half
            pltpu.make_async_copy(
                gq_in.at[p, side], gq_blk.at[:, at : at + half], load_sems.at[2]
            ).start()
    stores = [
        pltpu.make_async_copy(blocks[index], dst, store_sems.at[index])
        for index, dst in enumerate((gk_out, gv_out, gq_out))
    ]
    for index in range(3):
        pltpu.make_async_copy(blocks[index], blocks[index], load_sems.at[index]).wait()
        stores[index].start()
    for store in stores:
        store.wait()


def shards(queries, keys, values, grad_out, doc_lengths):
    n = lax.axis_size("tp")
    rows = queries.shape[0]
    block = rows * n
    wide = queries.shape[1] // n
    group = wide // HEAD
    blocks = 2 * FAR + 1
    bf16, f32 = jnp.bfloat16, jnp.float32
    vmem = pltpu.VMEM
    dma = pltpu.SemaphoreType.DMA
    any_spec = pl.BlockSpec(memory_space=pl.ANY)
    like_q = jax.ShapeDtypeStruct(queries.shape, bf16)
    like_k = jax.ShapeDtypeStruct(keys.shape, bf16)
    split_q = jax.ShapeDtypeStruct((n, 2, rows, wide // 2), bf16)
    split_kv = jax.ShapeDtypeStruct((n, 2, rows, HEAD), bf16)
    parts = pl.pallas_call(
        kernel,
        out_shape=[split_q, split_kv],
        in_specs=[any_spec] * 4 + [pl.BlockSpec(memory_space=pltpu.SMEM)],
        out_specs=[any_spec] * 2,
        scratch_shapes=[
            vmem((2, *queries.shape), bf16),
            vmem((2, *keys.shape), bf16),
            vmem((2, block, wide), bf16),
            vmem((2 * FAR + 2, 2, block, HEAD), bf16),
            vmem((blocks * group, block, block), f32),
            vmem((blocks * group, block, block), f32),
            vmem((blocks * group, 1, block), f32),
            vmem((1, block), jnp.int32),
            vmem((group, HEAD, block), f32),
            vmem((2, block, wide // 2), bf16),
            vmem((FAR + 1, 2, block, HEAD), f32),
            vmem((FAR, 2, block, HEAD), f32),
            vmem((FAR + 1, 2, block, HEAD), bf16),
            vmem((FAR + 1, 2, block, HEAD), bf16),
            vmem((FAR + 1, 2, block, HEAD), bf16),
            vmem((FAR, 2, block, HEAD), bf16),
            vmem((2, 2, block, HEAD), bf16),
            dma((4,)),
            dma((2,)),
            dma((5,)),
            dma((5,)),
            dma((FAR, 2, HALVES)),
            dma((FAR, 2, HALVES)),
            dma((FAR + 1, 2, HALVES)),
            dma((FAR + 1, 2, HALVES)),
            dma((FAR, 2, HALVES)),
            dma((FAR, 2, HALVES)),
            dma((2, 2, HALVES)),
            dma((2, 2, HALVES)),
            dma((FAR + 1,)),
            dma((FAR + 1,)),
            dma((4,)),
            dma((2,)),
        ],
        compiler_params=pltpu.CompilerParams(
            collective_id=0, has_side_effects=True, vmem_limit_bytes=60 * 2**20
        ),
    )(queries, keys, values, grad_out, doc_lengths)
    return pl.pallas_call(
        finish,
        out_shape=[like_q, like_k, like_k],
        in_specs=[any_spec] * 2,
        out_specs=[any_spec] * 3,
        scratch_shapes=[
            vmem(queries.shape, bf16),
            vmem((2, *keys.shape), bf16),
            dma((3,)),
            dma((3,)),
        ],
        compiler_params=pltpu.CompilerParams(vmem_limit_bytes=60 * 2**20),
    )(*parts)


def solution(mesh):
    placed = P(("ctx", "tp"), None)
    return jax.shard_map(
        shards,
        mesh=mesh,
        in_specs=(placed,) * 4 + (P(),),
        out_specs=(placed,) * 3,
        check_vma=False,
    )
```
